128 devices in a mesh: tm: 32 (over x, y, core), grp: 4 (over z).
Axes of the slice: x: 4, y: 4, z: 4, core: 2. Of those that a mesh axis runs over, the one named last changes fastest.
Arguments:
- init_field: float32 [256, 256], replicated, may hold values from -3 to 3
- reaction: float32 [256, 256], replicated, may hold values from 0.0003 to 0.0015
- guesses: float32 [128, 256, 256], P(('tm', 'grp')), may hold values from -3 to 3
Outputs:
- c_points: float32 [128, 256, 256], P(('tm', 'grp'))
- corners: float32 [32, 256, 256], P('tm')
The draws below stay inside these ranges and needn't reach their ends.
All inputs are finite; a program needn't handle non-finite values.
Results may differ from the reference program's by a relative error of at most 0.00002.
Values sent between devices are 32-bit elements; how exact they have to be, the bound alone decides.
A program may use at most 64 MiB of HBM per device.

```python
import math
import jax
import jax.numpy as jnp
from jax import lax

NX = 256
NY = 256
STEPS = 16
SLABS = 128
N_TM = 32
N_GRP = 4


def shard_levels(own_key, extent, shards, smallest, largest):
    loudness = 1.0
    for position, parts in shards:
        draws = jax.random.uniform(jax.random.fold_in(jax.random.fold_in(own_key, 6), position), (parts,), jnp.float32, smallest / len(shards), largest / len(shards))
        loudness = loudness * jnp.repeat(jnp.exp(draws), extent[position] // parts).reshape((-1,) + (1,) * (len(extent) - 1 - position))
    return loudness


def bell_draw(rng, dims, spread, most, pieces=(), kind=jnp.bfloat16):
    entries = spread * jax.random.normal(rng, dims, jnp.float32)
    if pieces:
        entries = entries * shard_levels(rng, dims, pieces, -0.22, 0.18)
    return jnp.clip(entries, -most, most).astype(kind)


def setup_inputs(seed: int = 0) -> dict:
    arg_keys = jax.random.split(jax.random.key(seed), 4)
    init_field = bell_draw(arg_keys[0], (NX, NY), 1.0, 3.0, (), jnp.float32)
    reaction = jnp.clip(jnp.exp(jax.random.uniform(arg_keys[1], (NX, NY), jnp.float32, math.log(0.0003), math.log(0.0015))), 0.0003, 0.0015)
    guesses = bell_draw(arg_keys[2], (SLABS, NX, NY), 1.0, 3.0, ((0, 128),), jnp.float32)
    return dict(init_field=init_field, reaction=reaction, guesses=guesses)


KAPPA = 0.0035


def advance(values, reaction, factor):
    beside = jnp.roll(values, 1, -2) + jnp.roll(values, -1, -2) + jnp.roll(values, 1, -1) + jnp.roll(values, -1, -1)
    return values + factor * (KAPPA * (beside - 4.0 * values) + reaction * (values - values * values * values))


def repeat(values, reaction, factor, count):
    return lax.fori_loop(0, count, lambda index, state: advance(state, reaction, factor), values)


def reference(init_field, reaction, guesses):
    members = N_GRP
    groups = N_TM
    fine_factor = float(STEPS)
    coarse_factor = float(STEPS * members)
    prior = jnp.concatenate([init_field[None], guesses[1:]], 0)
    relaxed = repeat(prior, reaction, 1.0, STEPS)
    start = jnp.concatenate([init_field[None], relaxed[:-1]], 0)
    terms = repeat(start, reaction, 1.0, STEPS) - advance(start, reaction, fine_factor)
    terms = terms.reshape(groups, members, NX, NY)
    ends = relaxed.reshape(groups, members, NX, NY)[:, members - 1]
    corner = jnp.concatenate([init_field[None], ends[:-1]], 0)
    for index in range(members):
        corner = advance(corner, reaction, fine_factor) + terms[:, index]
    fresh = jnp.concatenate([init_field[None], corner[:-1]], 0)
    composed = fresh
    for index in range(members):
        composed = advance(composed, reaction, fine_factor) + terms[:, index]
    coarse_term = composed - advance(fresh, reaction, coarse_factor)

    def chain_step(state, addend):
        following = advance(state, reaction, coarse_factor) + addend
        return following, following

    unused, after = lax.scan(chain_step, init_field, coarse_term)
    before = jnp.concatenate([init_field[None], after[:-1]], 0)
    points = []
    carried = before
    for index in range(members - 1):
        carried = advance(carried, reaction, fine_factor) + terms[:, index]
        points.append(carried)
    points.append(after)
    return (jnp.stack(points, 1).reshape(groups * members, NX, NY), corner)
```

```python
import functools

import jax
import jax.numpy as jnp
from jax import lax
from jax.experimental import pallas as pl
from jax.experimental.pallas import tpu as pltpu
from jax.sharding import PartitionSpec as P

STEPS = 16
KAPPA = 0.0035
MESH = pl.DeviceIdType.MESH

N = 256
LANES = 128
HALO = 40
CORE = 64
ROWS = CORE + 2 * HALO
M = ROWS // 8
MF = N // 8
STAGE = 16
F32 = jnp.float32


def at_xy(x, y, c):
    return (x * 4 + y) * 2 + c


def permutation(transposed):
    big = lax.broadcasted_iota(jnp.int32, (N, N), 1 if transposed else 0)
    new = lax.broadcasted_iota(jnp.int32, (N, N), 0 if transposed else 1)
    wanted = 2 * (new % LANES) + new // LANES
    return (big == wanted).astype(F32).astype(jnp.bfloat16)


def permuted(values, matrix):
    high = values.astype(jnp.bfloat16)
    rest = values - high.astype(F32)
    middle = rest.astype(jnp.bfloat16)
    low = (rest - middle.astype(F32)).astype(jnp.bfloat16)
    dot = functools.partial(jnp.dot, preferred_element_type=F32)
    return (dot(high, matrix) + dot(middle, matrix)) + dot(low, matrix)


def advance(state, a_ref, b_ref, scale):
    left, right = state
    m = len(left)
    new_left, new_right = [], []
    for k in range(m):
        u, v = left[k], right[k]
        above = [
            pltpu.roll(half[m - 1], 1, 0) if k == 0 else half[k - 1] for half in state
        ]
        below = [
            pltpu.roll(half[0], 7, 0) if k == m - 1 else half[k + 1] for half in state
        ]
        su = above[0] + below[0] + (v + pltpu.roll(v, 1, 1))
        sv = above[1] + below[1] + (u + pltpu.roll(u, LANES - 1, 1))
        new_left.append(scale * su + u * (a_ref[0, k] - b_ref[0, k] * (u * u)))
        new_right.append(scale * sv + v * (a_ref[1, k] - b_ref[1, k] * (v * v)))
    return new_left, new_right


def load_rows(ref, m):
    return [[ref[h, pl.ds(k, 8, stride=m), :] for k in range(m)] for h in range(2)]


def store_rows(ref, state, first=0):
    m = len(state[0])
    for h in range(2):
        for k in range(m):
            ref[h, pl.ds(first + k, 8, stride=m), :] = state[h][k]


def load_state(ref):
    return [[ref[h, k] for k in range(ref.shape[1])] for h in range(2)]


def store_state(ref, state):
    for h in range(2):
        for k in range(len(state[h])):
            ref[h, k] = state[h][k]


def plus(state, addend):
    return [[x + y for x, y in zip(s, t)] for s, t in zip(state, addend)]


def minus(state, addend):
    return [[x - y for x, y in zip(s, t)] for s, t in zip(state, addend)]


def repeat(state, a_ref, b_ref, scale, count, unroll):
    def turn(_, carried):
        carried = [list(half) for half in carried]
        for _ in range(unroll):
            carried = advance(carried, a_ref, b_ref, scale)
        return tuple(tuple(half) for half in carried)

    state = tuple(tuple(half) for half in state)
    state = lax.fori_loop(0, count // unroll, turn, state)
    return [list(half) for half in state]


def widen(ext, values):
    for h in range(2):
        part = values[:, h * LANES : (h + 1) * LANES]
        ext[h, HALO : HALO + N] = part
        ext[h, 0:HALO] = part[N - HALO :]
        ext[h, HALO + N :] = part[:HALO]


def copy_strip(dst, ext, first):
    for h in range(2):
        for row in range(0, ROWS, 8):
            src = pl.ds(pl.multiple_of(first + row, 8), 8)
            dst[h, row : row + 8] = ext[h, src]


def kernel(
    init_ref,
    rate_ref,
    guess_ref,
    points_ref,
    corner_ref,
    perm,
    init_ext,
    rate_ext,
    relaxed_ext,
    strip,
    a_full,
    b_full,
    a_1,
    b_1,
    a_16,
    b_16,
    a_64,
    b_64,
    starts,
    terms,
    corner_rows,
    corner_full,
    fresh,
    ct_rows,
    ct,
    cts,
    history,
    hop_rows,
    z_stage,
    pass_rows,
    z_in,
    z_own,
    point_rows,
    points_full,
    start_send,
    start_recv,
    corner_send,
    corner_recv,
    fresh_send,
    fresh_recv,
    ct_send,
    ct_recv,
    hop_send,
    hop_recv,
    pass_send,
    pass_recv,
    point_send,
    point_recv,
):
    group = lax.axis_index("tm")
    member = lax.axis_index("grp")
    groups = 32
    x, y, c = group // 8, (group // 2) % 4, group % 2
    stage = x // 2
    chip_x = x % 2
    local_group = group % STAGE
    core0 = c == 0

    def around(distance):
        return (member + distance) % 4

    barrier = pltpu.get_barrier_semaphore()

    def greet(tm, grp):
        pl.semaphore_signal(barrier, inc=1, device_id=(tm, grp), device_id_type=MESH)

    for d in (1, 2, 3):
        greet(group, around(d))

    @pl.when(group > 0)
    def _():
        greet(group - 1, 3)
        greet(group - 1, member)

    @pl.when(core0)
    def _():
        for dx in range(2):
            for dy in range(4):
                px, py = stage * 2 + (chip_x + dx) % 2, (y + dy) % 4
                if (dx, dy) != (0, 0):
                    greet(at_xy(px, py, 0), member)
                greet(at_xy(px, py, 1), member)

    @pl.when(jnp.logical_and(core0, stage == 1))
    def _():
        for d in (0, 1, 3):
            greet(at_xy(3 - x, y, 0), around(d))

    @pl.when(c == 1)
    def _():
        greet(group - 1, member)

    more = (group < groups - 1).astype(jnp.int32)
    expected = (
        3
        + more * (1 + 4 * (member == 3).astype(jnp.int32))
        + 7
        + c
        + (1 - c) * (1 + 3 * (1 - stage))
    )

    perm[...] = permutation(False)
    rate = permuted(rate_ref[...], perm[...])
    widen(rate_ext, rate)
    first = jnp.logical_and(group == 0, member == 0)
    prior = jnp.where(first, init_ref[...], guess_ref[0])
    widen(relaxed_ext, permuted(prior, perm[...]))
    full = relaxed_ext.at[:, HALO : HALO + N]
    rates = load_rows(rate_ext.at[:, HALO : HALO + N], MF)
    for h in range(2):
        for k in range(MF):
            a_full[h, k] = (1.0 - 4.0 * KAPPA) + rates[h][k]
            b_full[h, k] = rates[h][k]
    relaxed = repeat(load_rows(full, MF), a_full, b_full, KAPPA, STEPS, 4)
    store_rows(relaxed_ext, relaxed, HALO)
    for h in range(2):
        relaxed_ext[h, 0:HALO] = relaxed_ext[h, N : N + HALO]
        relaxed_ext[h, HALO + N :] = relaxed_ext[h, HALO : 2 * HALO]

    pl.semaphore_wait(barrier, expected)

    pending = []
    slot = (member + 1) % 4
    target = group + (member == 3).astype(jnp.int32)
    have = jnp.logical_or(member < 3, group < groups - 1)
    for d in (1, 3, 2, 0):
        q = around(d)
        copy = pltpu.make_async_remote_copy(
            src_ref=relaxed_ext.at[:, pl.ds(pl.multiple_of(q * CORE, 8), ROWS)],
            dst_ref=starts.at[slot],
            send_sem=start_send.at[d],
            recv_sem=start_recv.at[slot],
            device_id=(target, q),
            device_id_type=MESH,
        )
        when = have if d else jnp.logical_and(have, member == 3)
        pl.when(when)(copy.start)
        pending.append((when, copy))

    own_first = pl.multiple_of(member * CORE, 8)

    @pl.when(member < 3)
    def _():
        copy_strip(starts.at[slot], relaxed_ext, own_first)

    widen(init_ext, permuted(init_ref[...], perm[...]))

    @pl.when(group == 0)
    def _():
        copy_strip(starts.at[0], init_ext, own_first)
        copy_strip(fresh, init_ext, own_first)

    copy_strip(strip, rate_ext, own_first)
    rates = load_rows(strip, M)
    for h in range(2):
        for k in range(M):
            r = rates[h][k]
            for factor, a_ref, b_ref in (
                (1.0, a_1, b_1),
                (16.0, a_16, b_16),
                (64.0, a_64, b_64),
            ):
                a_ref[h, k] = (1.0 - 4.0 * KAPPA * factor) + factor * r
                b_ref[h, k] = factor * r
    copy_strip(strip, init_ext, own_first)
    perm[...] = permutation(True)

    def one_term(turn, _):
        offset = turn + (turn == 2).astype(jnp.int32) - (turn == 3).astype(jnp.int32)
        s = (member + 1 + offset) % 4
        remote = jnp.where(s == 0, group > 0, s != member + 1)

        @pl.when(remote)
        def _():
            pltpu.make_async_remote_copy(
                src_ref=starts.at[s],
                dst_ref=starts.at[s],
                send_sem=start_send.at[0],
                recv_sem=start_recv.at[s],
                device_id=(group, around(1)),
                device_id_type=MESH,
            ).wait_recv()

        start = load_rows(starts.at[s], M)
        store_state(terms.at[s], advance(start, a_16, b_16, 16.0 * KAPPA))
        fine = repeat(load_rows(starts.at[s], M), a_1, b_1, KAPPA, STEPS, 4)
        store_state(terms.at[s], minus(fine, load_state(terms.at[s])))
        return 0

    lax.fori_loop(0, 4, one_term, 0)

    def big_step(state, index):
        stepped = advance(state, a_16, b_16, 16.0 * KAPPA)
        return plus(stepped, load_state(terms.at[index]))

    corner = load_rows(starts.at[0], M)
    for index in range(4):
        corner = big_step(corner, index)
    store_rows(corner_rows, corner)
    sent = slice(HALO - 24, HALO + CORE + 24)
    copy = pltpu.make_async_remote_copy(
        src_ref=corner_rows.at[:, sent],
        dst_ref=fresh.at[:, sent],
        send_sem=fresh_send,
        recv_sem=fresh_recv,
        device_id=(lax.rem(group + 1, groups), member),
        device_id_type=MESH,
    )
    fresh_copy = copy
    pl.when(group < groups - 1)(copy.start)
    pending.append((group < groups - 1, copy))
    core_rows = slice(HALO, HALO + CORE)
    own_rows = pl.ds(own_first, CORE)
    for d in (1, 3, 2):
        copy = pltpu.make_async_remote_copy(
            src_ref=corner_rows.at[:, core_rows],
            dst_ref=corner_full.at[:, own_rows],
            send_sem=corner_send.at[d - 1],
            recv_sem=corner_recv.at[member],
            device_id=(group, around(d)),
            device_id_type=MESH,
        )
        copy.start()
        pending.append((None, copy))
    for h in range(2):
        corner_full[h, own_rows] = corner_rows[h, core_rows]

    pl.when(group > 0)(fresh_copy.wait_recv)
    state = load_rows(fresh, M)
    for index in range(4):
        state = big_step(state, index)
    state = minus(state, advance(load_rows(fresh, M), a_64, b_64, 64.0 * KAPPA))
    store_state(ct, state)
    store_rows(ct_rows, state)
    for dx in (1, 0):
        for dy in (2, 1, 3, 0):
            px, py = stage * 2 + (chip_x + dx) % 2, (y + dy) % 4
            copy = pltpu.make_async_remote_copy(
                src_ref=ct_rows.at[:, sent],
                dst_ref=cts.at[local_group, :, sent],
                send_sem=ct_send.at[dx * 4 + dy],
                recv_sem=ct_recv.at[local_group],
                device_id=(at_xy(px, py, 0), member),
                device_id_type=MESH,
            )
            when = None if (dx, dy) != (0, 0) else c == 1
            if when is None:
                copy.start()
            else:
                pl.when(when)(copy.start)
            pending.append((when, copy))

    for d in (1, 3, 2):
        q = around(d)
        pltpu.make_async_remote_copy(
            src_ref=corner_rows.at[:, core_rows],
            dst_ref=corner_full.at[:, pl.ds(pl.multiple_of(q * CORE, 8), CORE)],
            send_sem=corner_send.at[0],
            recv_sem=corner_recv.at[q],
            device_id=(group, q),
            device_id_type=MESH,
        ).wait_recv()
    both = jnp.concatenate([corner_full[0], corner_full[1]], axis=1)
    corner_ref[0] = permuted(both, perm[...])

    hop = []
    rows = 24
    for d, src, dst in (
        (3, HALO, HALO + CORE),
        (1, HALO + CORE - rows, HALO - rows),
        (0, HALO, HALO),
    ):
        count = rows if d else CORE
        hop.append(
            pltpu.make_async_remote_copy(
                src_ref=hop_rows.at[:, src : src + count],
                dst_ref=z_stage.at[:, dst : dst + count],
                send_sem=hop_send.at[d],
                recv_sem=hop_recv.at[d],
                device_id=(at_xy(3 - x, y, 0), around(d)),
                device_id_type=MESH,
            )
        )
    handed = slice(HALO - 8, HALO + CORE + 8)
    pass_copy = pltpu.make_async_remote_copy(
        src_ref=pass_rows.at[:, handed],
        dst_ref=z_in.at[:, handed],
        send_sem=pass_send,
        recv_sem=pass_recv,
        device_id=(at_xy(x, y, 1), member),
        device_id_type=MESH,
    )

    @pl.when(core0)
    def _():
        store_rows(cts.at[local_group], load_state(ct))

        @pl.when(stage == 0)
        def _():
            store_state(history.at[0], load_rows(strip, M))

        @pl.when(stage == 1)
        def _():
            for copy in hop:
                copy.wait_recv()
            store_state(history.at[0], load_rows(z_stage, M))

        def one_group(t, state):
            @pl.when(t != local_group)
            def _():
                pltpu.make_async_remote_copy(
                    src_ref=ct_rows.at[:, sent],
                    dst_ref=cts.at[t, :, sent],
                    send_sem=ct_send.at[0],
                    recv_sem=ct_recv.at[t],
                    device_id=(group, around(1)),
                    device_id_type=MESH,
                ).wait_recv()

            state = [list(half) for half in state]
            state = advance(state, a_64, b_64, 64.0 * KAPPA)
            state = plus(state, load_rows(cts.at[t], M))
            store_state(history.at[t + 1], state)
            return tuple(tuple(half) for half in state)

        begin = tuple(tuple(half) for half in load_state(history.at[0]))
        last = lax.fori_loop(0, STAGE, one_group, begin)

        @pl.when(stage == 0)
        def _():
            store_rows(hop_rows, last)
            for copy in hop:
                copy.start()

        store_rows(pass_rows, load_state(history.at[local_group + 1]))
        pass_copy.start()
        store_state(z_own, load_state(history.at[local_group]))

    @pl.when(c == 1)
    def _():
        pass_copy.wait_recv()
        store_state(z_own, load_rows(z_in, M))

    final = load_state(z_own)
    final = plus(advance(final, a_64, b_64, 64.0 * KAPPA), load_state(ct))
    state = load_state(z_own)
    for index in range(4):
        state = big_step(state, index) if index < 3 else final
        store_rows(point_rows.at[index], state)

        copy = pltpu.make_async_remote_copy(
            src_ref=point_rows.at[index, :, core_rows],
            dst_ref=points_full.at[:, own_rows],
            send_sem=point_send.at[index],
            recv_sem=point_recv.at[member],
            device_id=(group, index),
            device_id_type=MESH,
        )
        when = member != index
        pl.when(when)(copy.start)
        pending.append((when, copy))
    for h in range(2):
        points_full[h, own_rows] = point_rows[member, h, core_rows]
    for d in (1, 3, 2):
        q = around(d)
        pltpu.make_async_remote_copy(
            src_ref=point_rows.at[0, :, core_rows],
            dst_ref=points_full.at[:, pl.ds(pl.multiple_of(q * CORE, 8), CORE)],
            send_sem=point_send.at[0],
            recv_sem=point_recv.at[q],
            device_id=(group, q),
            device_id_type=MESH,
        ).wait_recv()
    both = jnp.concatenate([points_full[0], points_full[1]], axis=1)
    points_ref[0] = permuted(both, perm[...])

    for when, copy in pending:
        if when is None:
            copy.wait_send()
        else:
            pl.when(when)(copy.wait_send)

    @pl.when(core0)
    def _():
        pass_copy.wait_send()

        @pl.when(stage == 0)
        def _():
            for copy in hop:
                copy.wait_send()


def local(init_field, reaction, guesses):
    vmem = pl.BlockSpec(memory_space=pltpu.VMEM)
    strip_state = pltpu.VMEM((2, M, 8, LANES), F32)
    full_state = pltpu.VMEM((2, MF, 8, LANES), F32)
    strip_rows = pltpu.VMEM((2, ROWS, LANES), F32)
    ext_rows = pltpu.VMEM((2, N + 2 * HALO, LANES), F32)
    full_rows = pltpu.VMEM((2, N, LANES), F32)
    dma = pltpu.SemaphoreType.DMA

    def many(count, *shape):
        return pltpu.VMEM((count, *shape), F32)

    scratch = [
        pltpu.VMEM((N, N), jnp.bfloat16),
        ext_rows,
        ext_rows,
        ext_rows,
        strip_rows,
        full_state,
        full_state,
        *[strip_state] * 6,
        many(4, 2, ROWS, LANES),
        many(4, 2, M, 8, LANES),
        strip_rows,
        full_rows,
        strip_rows,
        strip_rows,
        strip_state,
        many(STAGE, 2, ROWS, LANES),
        many(STAGE + 1, 2, M, 8, LANES),
        strip_rows,
        strip_rows,
        strip_rows,
        strip_rows,
        strip_state,
        many(4, 2, ROWS, LANES),
        full_rows,
        dma((4,)),
        dma((4,)),
        dma((3,)),
        dma((4,)),
        dma,
        dma,
        dma((8,)),
        dma((STAGE,)),
        dma((4,)),
        dma((4,)),
        dma,
        dma,
        dma((4,)),
        dma((4,)),
    ]
    block = jax.ShapeDtypeStruct((1, N, N), F32)
    return pl.pallas_call(
        kernel,
        out_shape=(block, block),
        in_specs=[vmem] * 3,
        out_specs=(vmem, vmem),
        scratch_shapes=scratch,
        compiler_params=pltpu.CompilerParams(
            collective_id=0, has_side_effects=True, vmem_limit_bytes=32 * 2**20
        ),
    )(init_field, reaction, guesses)


def solution(mesh):
    return jax.shard_map(
        local,
        mesh=mesh,
        in_specs=(P(), P(), P(("tm", "grp"), None, None)),
        out_specs=(P(("tm", "grp"), None, None), P("tm", None, None)),
        check_vma=False,
    )
```

```python
import functools

import jax
import jax.numpy as jnp
from jax import lax
from jax.experimental import pallas as pl
from jax.experimental.pallas import tpu as pltpu
from jax.sharding import PartitionSpec as P

STEPS = 16
KAPPA = 0.0035
MESH = pl.DeviceIdType.MESH

N = 256
LANES = 128
HALO = 40
CORE = 64
ROWS = CORE + 2 * HALO
M = ROWS // 8
MF = N // 8
STAGE = 16
F32 = jnp.float32


def at_xy(x, y, c):
    return (x * 4 + y) * 2 + c


def permutation(transposed):
    big = lax.broadcasted_iota(jnp.int32, (N, N), 1 if transposed else 0)
    new = lax.broadcasted_iota(jnp.int32, (N, N), 0 if transposed else 1)
    wanted = 2 * (new % LANES) + new // LANES
    return (big == wanted).astype(F32).astype(jnp.bfloat16)


def permuted(values, matrix):
    high = values.astype(jnp.bfloat16)
    rest = values - high.astype(F32)
    middle = rest.astype(jnp.bfloat16)
    low = (rest - middle.astype(F32)).astype(jnp.bfloat16)
    dot = functools.partial(jnp.dot, preferred_element_type=F32)
    return (dot(high, matrix) + dot(middle, matrix)) + dot(low, matrix)


def advance(state, a_ref, b_ref, scale):
    left, right = state
    m = len(left)
    new_left, new_right = [], []
    for k in range(m):
        u, v = left[k], right[k]
        above = [
            pltpu.roll(half[m - 1], 1, 0) if k == 0 else half[k - 1] for half in state
        ]
        below = [
            pltpu.roll(half[0], 7, 0) if k == m - 1 else half[k + 1] for half in state
        ]
        su = above[0] + below[0] + (v + pltpu.roll(v, 1, 1))
        sv = above[1] + below[1] + (u + pltpu.roll(u, LANES - 1, 1))
        new_left.append(scale * su + u * (a_ref[0, k] - b_ref[0, k] * (u * u)))
        new_right.append(scale * sv + v * (a_ref[1, k] - b_ref[1, k] * (v * v)))
    return new_left, new_right


def load_rows(ref, m):
    return [[ref[h, pl.ds(k, 8, stride=m), :] for k in range(m)] for h in range(2)]


def store_rows(ref, state, first=0):
    m = len(state[0])
    for h in range(2):
        for k in range(m):
            ref[h, pl.ds(first + k, 8, stride=m), :] = state[h][k]


def load_state(ref):
    return [[ref[h, k] for k in range(ref.shape[1])] for h in range(2)]


def store_state(ref, state):
    for h in range(2):
        for k in range(len(state[h])):
            ref[h, k] = state[h][k]


def plus(state, addend):
    return [[x + y for x, y in zip(s, t)] for s, t in zip(state, addend)]


def minus(state, addend):
    return [[x - y for x, y in zip(s, t)] for s, t in zip(state, addend)]


def repeat(state, a_ref, b_ref, scale, count, unroll):
    def turn(_, carried):
        carried = [list(half) for half in carried]
        for _ in range(unroll):
            carried = advance(carried, a_ref, b_ref, scale)
        return tuple(tuple(half) for half in carried)

    state = tuple(tuple(half) for half in state)
    state = lax.fori_loop(0, count // unroll, turn, state)
    return [list(half) for half in state]


def widen(ext, values):
    for h in range(2):
        part = values[:, h * LANES : (h + 1) * LANES]
        ext[h, HALO : HALO + N] = part
        ext[h, 0:HALO] = part[N - HALO :]
        ext[h, HALO + N :] = part[:HALO]


def copy_strip(dst, ext, first):
    for h in range(2):
        for row in range(0, ROWS, 8):
            src = pl.ds(pl.multiple_of(first + row, 8), 8)
            dst[h, row : row + 8] = ext[h, src]


def kernel(
    init_ref,
    rate_ref,
    guess_ref,
    points_full,
    corner_ref,
    init_in,
    rate_in,
    prior_in,
    perm,
    init_ext,
    rate_ext,
    relaxed_ext,
    strip,
    a_full,
    b_full,
    a_1,
    b_1,
    a_16,
    b_16,
    a_64,
    b_64,
    starts,
    terms,
    corner_rows,
    corner_full,
    fresh,
    ct_rows,
    ct,
    cts,
    history,
    hop_rows,
    z_stage,
    pass_rows,
    z_in,
    z_own,
    point_rows,
    in_sem,
    start_send,
    start_recv,
    corner_send,
    corner_recv,
    fresh_send,
    fresh_recv,
    ct_send,
    ct_recv,
    hop_send,
    hop_recv,
    pass_send,
    pass_recv,
    point_send,
    point_recv,
):
    group = lax.axis_index("tm")
    member = lax.axis_index("grp")
    groups = 32
    x, y, c = group // 8, (group // 2) % 4, group % 2
    stage = x // 2
    chip_x = x % 2
    local_group = group % STAGE
    core0 = c == 0

    def around(distance):
        return (member + distance) % 4

    first = jnp.logical_and(group == 0, member == 0)
    rate_copy = pltpu.make_async_copy(rate_ref, rate_in, in_sem.at[0])
    rate_copy.start()
    prior_copies = (
        pltpu.make_async_copy(init_ref, prior_in, in_sem.at[1]),
        pltpu.make_async_copy(guess_ref.at[0], prior_in, in_sem.at[1]),
    )
    pl.when(first)(prior_copies[0].start)
    pl.when(jnp.logical_not(first))(prior_copies[1].start)
    init_copy = pltpu.make_async_copy(init_ref, init_in, in_sem.at[2])
    init_copy.start()

    barrier = pltpu.get_barrier_semaphore()

    def greet(tm, grp):
        pl.semaphore_signal(barrier, inc=1, device_id=(tm, grp), device_id_type=MESH)

    for d in (1, 2, 3):
        greet(group, around(d))

    @pl.when(group > 0)
    def _():
        greet(group - 1, 3)
        greet(group - 1, member)

    @pl.when(core0)
    def _():
        for dx in range(2):
            for dy in range(4):
                px, py = stage * 2 + (chip_x + dx) % 2, (y + dy) % 4
                if (dx, dy) != (0, 0):
                    greet(at_xy(px, py, 0), member)
                greet(at_xy(px, py, 1), member)

    @pl.when(jnp.logical_and(core0, stage == 1))
    def _():
        for d in (0, 1, 3):
            greet(at_xy(3 - x, y, 0), around(d))

    @pl.when(c == 1)
    def _():
        greet(group - 1, member)

    more = (group < groups - 1).astype(jnp.int32)
    expected = (
        3
        + more * (1 + 4 * (member == 3).astype(jnp.int32))
        + 7
        + c
        + (1 - c) * (1 + 3 * (1 - stage))
    )

    perm[...] = permutation(False)
    rate_copy.wait()
    rate = permuted(rate_in[...], perm[...])
    widen(rate_ext, rate)
    prior_copies[1].wait()
    prior = permuted(prior_in[...], perm[...])
    for h in range(2):
        relaxed_ext[h, HALO : HALO + N] = prior[:, h * LANES : (h + 1) * LANES]
    full = relaxed_ext.at[:, HALO : HALO + N]
    rates = load_rows(rate_ext.at[:, HALO : HALO + N], MF)
    for h in range(2):
        for k in range(MF):
            a_full[h, k] = (1.0 - 4.0 * KAPPA) + rates[h][k]
            b_full[h, k] = rates[h][k]
    relaxed = repeat(load_rows(full, MF), a_full, b_full, KAPPA, STEPS, 4)
    store_rows(relaxed_ext, relaxed, HALO)
    for h in range(2):
        relaxed_ext[h, 0:HALO] = relaxed_ext[h, N : N + HALO]
        relaxed_ext[h, HALO + N :] = relaxed_ext[h, HALO : 2 * HALO]

    pl.semaphore_wait(barrier, expected)

    pending = []
    slot = (member + 1) % 4
    target = group + (member == 3).astype(jnp.int32)
    have = jnp.logical_or(member < 3, group < groups - 1)
    for d in (1, 3, 2, 0):
        q = around(d)
        copy = pltpu.make_async_remote_copy(
            src_ref=relaxed_ext.at[:, pl.ds(pl.multiple_of(q * CORE, 8), ROWS)],
            dst_ref=starts.at[slot],
            send_sem=start_send.at[d],
            recv_sem=start_recv.at[slot],
            device_id=(target, q),
            device_id_type=MESH,
        )
        when = have if d else jnp.logical_and(have, member == 3)
        pl.when(when)(copy.start)
        pending.append((when, copy))

    own_first = pl.multiple_of(member * CORE, 8)

    @pl.when(member < 3)
    def _():
        copy_strip(starts.at[slot], relaxed_ext, own_first)

    init_copy.wait()
    widen(init_ext, permuted(init_in[...], perm[...]))

    @pl.when(group == 0)
    def _():
        copy_strip(starts.at[0], init_ext, own_first)
        copy_strip(fresh, init_ext, own_first)

    copy_strip(strip, rate_ext, own_first)
    rates = load_rows(strip, M)
    for h in range(2):
        for k in range(M):
            r = rates[h][k]
            for factor, a_ref, b_ref in (
                (1.0, a_1, b_1),
                (16.0, a_16, b_16),
                (64.0, a_64, b_64),
            ):
                a_ref[h, k] = (1.0 - 4.0 * KAPPA * factor) + factor * r
                b_ref[h, k] = factor * r
    copy_strip(strip, init_ext, own_first)
    perm[...] = permutation(True)

    def make_terms(slots):
        for s in slots:
            remote = jnp.where(s == 0, group > 0, s != member + 1)

            @pl.when(remote)
            def _(s=s):
                pltpu.make_async_remote_copy(
                    src_ref=starts.at[s],
                    dst_ref=starts.at[s],
                    send_sem=start_send.at[0],
                    recv_sem=start_recv.at[s],
                    device_id=(group, around(1)),
                    device_id_type=MESH,
                ).wait_recv()

        for s in slots:
            start = load_rows(starts.at[s], M)
            store_state(terms.at[s], advance(start, a_16, b_16, 16.0 * KAPPA))

        def turn(_, carried):
            for _ in range(4):
                carried = [advance(state, a_1, b_1, KAPPA) for state in carried]
            return tuple(tuple(tuple(half) for half in state) for state in carried)

        carried = tuple(
            tuple(tuple(half) for half in load_rows(starts.at[s], M)) for s in slots
        )
        fine = lax.fori_loop(0, STEPS // 4, turn, carried)
        for s, state in zip(slots, fine):
            store_state(terms.at[s], minus(state, load_state(terms.at[s])))

    make_terms([slot])
    make_terms([(slot + 1) % 4, (slot + 3) % 4])
    make_terms([(slot + 2) % 4])

    def big_step(state, index):
        stepped = advance(state, a_16, b_16, 16.0 * KAPPA)
        return plus(stepped, load_state(terms.at[index]))

    corner = load_rows(starts.at[0], M)
    for index in range(4):
        corner = big_step(corner, index)
    store_rows(corner_rows, corner)
    sent = slice(HALO - 24, HALO + CORE + 24)
    copy = pltpu.make_async_remote_copy(
        src_ref=corner_rows.at[:, sent],
        dst_ref=fresh.at[:, sent],
        send_sem=fresh_send,
        recv_sem=fresh_recv,
        device_id=(lax.rem(group + 1, groups), member),
        device_id_type=MESH,
    )
    fresh_copy = copy
    pl.when(group < groups - 1)(copy.start)
    pending.append((group < groups - 1, copy))
    core_rows = slice(HALO, HALO + CORE)
    own_rows = pl.ds(own_first, CORE)
    for d in (1, 3, 2):
        copy = pltpu.make_async_remote_copy(
            src_ref=corner_rows.at[:, core_rows],
            dst_ref=corner_full.at[:, own_rows],
            send_sem=corner_send.at[d - 1],
            recv_sem=corner_recv.at[member],
            device_id=(group, around(d)),
            device_id_type=MESH,
        )
        copy.start()
        pending.append((None, copy))
    for h in range(2):
        corner_full[h, own_rows] = corner_rows[h, core_rows]

    pl.when(group > 0)(fresh_copy.wait_recv)
    state = load_rows(fresh, M)
    for index in range(4):
        state = big_step(state, index)
    state = minus(state, advance(load_rows(fresh, M), a_64, b_64, 64.0 * KAPPA))
    store_state(ct, state)
    store_rows(ct_rows, state)
    def ct_copies(halo):
        rows = slice(HALO - halo, HALO + CORE + halo)
        copies = []
        for dx in (1, 0):
            for dy in (2, 1, 3, 0):
                px, py = stage * 2 + (chip_x + dx) % 2, (y + dy) % 4
                copies.append(
                    pltpu.make_async_remote_copy(
                        src_ref=ct_rows.at[:, rows],
                        dst_ref=cts.at[local_group, :, rows],
                        send_sem=ct_send.at[dx * 4 + dy],
                        recv_sem=ct_recv.at[local_group],
                        device_id=(at_xy(px, py, 0), member),
                        device_id_type=MESH,
                    )
                )
        return copies

    widths = (
        (24, local_group == 0),
        (16, jnp.logical_and(local_group > 0, local_group <= 8)),
        (8, local_group > 8),
    )
    for halo, when in widths:

        @pl.when(when)
        def _(halo=halo):
            copies = ct_copies(halo)
            for copy in copies[:-1]:
                copy.start()
            pl.when(c == 1)(copies[-1].start)

    for d in (1, 3, 2):
        q = around(d)
        pltpu.make_async_remote_copy(
            src_ref=corner_rows.at[:, core_rows],
            dst_ref=corner_full.at[:, pl.ds(pl.multiple_of(q * CORE, 8), CORE)],
            send_sem=corner_send.at[0],
            recv_sem=corner_recv.at[q],
            device_id=(group, q),
            device_id_type=MESH,
        ).wait_recv()
    both = jnp.concatenate([corner_full[0], corner_full[1]], axis=1)
    corner_ref[...] = permuted(both, perm[...])

    hop = []
    rows = 24
    for d, src, dst in (
        (3, HALO, HALO + CORE),
        (1, HALO + CORE - rows, HALO - rows),
        (0, HALO, HALO),
    ):
        count = rows if d else CORE
        hop.append(
            pltpu.make_async_remote_copy(
                src_ref=hop_rows.at[:, src : src + count],
                dst_ref=z_stage.at[:, dst : dst + count],
                send_sem=hop_send.at[d],
                recv_sem=hop_recv.at[d],
                device_id=(at_xy(3 - x, y, 0), around(d)),
                device_id_type=MESH,
            )
        )
    handed = slice(HALO - 8, HALO + CORE + 8)
    pass_copy = pltpu.make_async_remote_copy(
        src_ref=pass_rows.at[:, handed],
        dst_ref=z_in.at[:, handed],
        send_sem=pass_send,
        recv_sem=pass_recv,
        device_id=(at_xy(x, y, 1), member),
        device_id_type=MESH,
    )

    @pl.when(core0)
    def _():
        store_rows(cts.at[local_group], load_state(ct))

        @pl.when(stage == 0)
        def _():
            store_state(history.at[0], load_rows(strip, M))

        @pl.when(stage == 1)
        def _():
            for copy in hop:
                copy.wait_recv()
            store_state(history.at[0], load_rows(z_stage, M))

        last = load_state(history.at[0])
        for t in range(STAGE):
            if t % 4 == 0:
                for n in range(t, t + 4):
                    halo = 24 if n == 0 else 16 if n <= 8 else 8
                    rows = slice(HALO - halo, HALO + CORE + halo)

                    @pl.when(n != local_group)
                    def _(n=n, rows=rows):
                        pltpu.make_async_remote_copy(
                            src_ref=ct_rows.at[:, rows],
                            dst_ref=cts.at[n, :, rows],
                            send_sem=ct_send.at[0],
                            recv_sem=ct_recv.at[n],
                            device_id=(group, around(1)),
                            device_id_type=MESH,
                        ).wait_recv()

            last = advance(last, a_64, b_64, 64.0 * KAPPA)
            last = plus(last, load_rows(cts.at[t], M))
            store_state(history.at[t + 1], last)

        @pl.when(stage == 0)
        def _():
            store_rows(hop_rows, last)
            for copy in hop:
                copy.start()

        store_rows(pass_rows, load_state(history.at[local_group + 1]))
        pass_copy.start()
        store_state(z_own, load_state(history.at[local_group]))

    @pl.when(c == 1)
    def _():
        pass_copy.wait_recv()
        store_state(z_own, load_rows(z_in, M))

    final = load_state(z_own)
    final = plus(advance(final, a_64, b_64, 64.0 * KAPPA), load_state(ct))
    state = load_state(z_own)
    for index in (3, 0, 1, 2):
        if index < 3:
            state = big_step(state, index)
        store_rows(point_rows.at[index], state if index < 3 else final)

        copy = pltpu.make_async_remote_copy(
            src_ref=point_rows.at[index, :, core_rows],
            dst_ref=points_full.at[:, own_rows],
            send_sem=point_send.at[index],
            recv_sem=point_recv.at[member],
            device_id=(group, index),
            device_id_type=MESH,
        )
        when = member != index
        pl.when(when)(copy.start)
        pending.append((when, copy))
    for h in range(2):
        points_full[h, own_rows] = point_rows[member, h, core_rows]
    for d in (1, 3, 2):
        q = around(d)
        pltpu.make_async_remote_copy(
            src_ref=point_rows.at[0, :, core_rows],
            dst_ref=points_full.at[:, pl.ds(pl.multiple_of(q * CORE, 8), CORE)],
            send_sem=point_send.at[0],
            recv_sem=point_recv.at[q],
            device_id=(group, q),
            device_id_type=MESH,
        ).wait_recv()

    for when, copy in pending:
        if when is None:
            copy.wait_send()
        else:
            pl.when(when)(copy.wait_send)

    for halo, when in widths:

        @pl.when(when)
        def _(halo=halo):
            copies = ct_copies(halo)
            for copy in copies[:-1]:
                copy.wait_send()
            pl.when(c == 1)(copies[-1].wait_send)

    @pl.when(core0)
    def _():
        pass_copy.wait_send()

        @pl.when(stage == 0)
        def _():
            for copy in hop:
                copy.wait_send()


def write_out(points_full, corner, points_out, corner_out, rows, sems):
    corner_copy = pltpu.make_async_copy(corner, corner_out.at[0], sems.at[0])
    corner_copy.start()
    matrix = permutation(True)
    copies = [corner_copy]
    for part in range(2):
        some = slice(part * LANES, (part + 1) * LANES)
        both = jnp.concatenate([points_full[0, some], points_full[1, some]], axis=1)
        rows[some] = permuted(both, matrix)
        copy = pltpu.make_async_copy(
            rows.at[some], points_out.at[0, some], sems.at[1 + part]
        )
        copy.start()
        copies.append(copy)
    for copy in copies:
        copy.wait()


def local(init_field, reaction, guesses):
    vmem = pl.BlockSpec(memory_space=pltpu.VMEM)
    strip_state = pltpu.VMEM((2, M, 8, LANES), F32)
    full_state = pltpu.VMEM((2, MF, 8, LANES), F32)
    strip_rows = pltpu.VMEM((2, ROWS, LANES), F32)
    ext_rows = pltpu.VMEM((2, N + 2 * HALO, LANES), F32)
    full_rows = pltpu.VMEM((2, N, LANES), F32)
    dma = pltpu.SemaphoreType.DMA

    def many(count, *shape):
        return pltpu.VMEM((count, *shape), F32)

    scratch = [
        *[pltpu.VMEM((N, N), F32)] * 3,
        pltpu.VMEM((N, N), jnp.bfloat16),
        ext_rows,
        ext_rows,
        ext_rows,
        strip_rows,
        full_state,
        full_state,
        *[strip_state] * 6,
        many(4, 2, ROWS, LANES),
        many(4, 2, M, 8, LANES),
        strip_rows,
        full_rows,
        strip_rows,
        strip_rows,
        strip_state,
        many(STAGE, 2, ROWS, LANES),
        many(STAGE + 1, 2, M, 8, LANES),
        strip_rows,
        strip_rows,
        strip_rows,
        strip_rows,
        strip_state,
        many(4, 2, ROWS, LANES),
        dma((3,)),
        dma((4,)),
        dma((4,)),
        dma((3,)),
        dma((4,)),
        dma,
        dma,
        dma((8,)),
        dma((STAGE,)),
        dma((4,)),
        dma((4,)),
        dma,
        dma,
        dma((4,)),
        dma((4,)),
    ]
    hbm = pl.BlockSpec(memory_space=pltpu.HBM)
    points, corner = pl.pallas_call(
        kernel,
        out_shape=(
            jax.ShapeDtypeStruct((2, N, LANES), F32),
            jax.ShapeDtypeStruct((N, N), F32),
        ),
        in_specs=[hbm] * 3,
        out_specs=(vmem, vmem),
        scratch_shapes=scratch,
        compiler_params=pltpu.CompilerParams(
            collective_id=0, has_side_effects=True, vmem_limit_bytes=213 * 2**18
        ),
    )(init_field, reaction, guesses)
    block = jax.ShapeDtypeStruct((1, N, N), F32)
    return pl.pallas_call(
        write_out,
        out_shape=(block, block),
        in_specs=[vmem] * 2,
        out_specs=(hbm, hbm),
        scratch_shapes=[pltpu.VMEM((N, N), F32), dma((3,))],
        compiler_params=pltpu.CompilerParams(vmem_limit_bytes=8 * 2**20),
    )(points, corner)


def solution(mesh):
    return jax.shard_map(
        local,
        mesh=mesh,
        in_specs=(P(), P(), P(("tm", "grp"), None, None)),
        out_specs=(P(("tm", "grp"), None, None), P("tm", None, None)),
        check_vma=False,
    )
```

```python
import functools

import jax
import jax.numpy as jnp
from jax import lax
from jax.experimental import pallas as pl
from jax.experimental.pallas import tpu as pltpu
from jax.sharding import PartitionSpec as P

STEPS = 16
KAPPA = 0.0035
MESH = pl.DeviceIdType.MESH

N = 256
LANES = 128
HALO = 40
CORE = 64
ROWS = CORE + 2 * HALO
M = ROWS // 8
MF = N // 8
STAGE = 16
F32 = jnp.float32


def at_xy(x, y, c):
    return (x * 4 + y) * 2 + c


def permutation(transposed):
    big = lax.broadcasted_iota(jnp.int32, (N, N), 1 if transposed else 0)
    new = lax.broadcasted_iota(jnp.int32, (N, N), 0 if transposed else 1)
    wanted = 2 * (new % LANES) + new // LANES
    return (big == wanted).astype(F32).astype(jnp.bfloat16)


def permuted(values, matrix):
    high = values.astype(jnp.bfloat16)
    rest = values - high.astype(F32)
    middle = rest.astype(jnp.bfloat16)
    low = (rest - middle.astype(F32)).astype(jnp.bfloat16)
    dot = functools.partial(jnp.dot, preferred_element_type=F32)
    return (dot(high, matrix) + dot(middle, matrix)) + dot(low, matrix)


def advance(state, a_ref, b_ref, scale):
    left, right = state
    m = len(left)
    new_left, new_right = [], []
    for k in range(m):
        u, v = left[k], right[k]
        above = [
            pltpu.roll(half[m - 1], 1, 0) if k == 0 else half[k - 1] for half in state
        ]
        below = [
            pltpu.roll(half[0], 7, 0) if k == m - 1 else half[k + 1] for half in state
        ]
        su = above[0] + below[0] + (v + pltpu.roll(v, 1, 1))
        sv = above[1] + below[1] + (u + pltpu.roll(u, LANES - 1, 1))
        new_left.append(scale * su + u * (a_ref[0, k] - b_ref[0, k] * (u * u)))
        new_right.append(scale * sv + v * (a_ref[1, k] - b_ref[1, k] * (v * v)))
    return new_left, new_right


def load_rows(ref, m):
    return [[ref[h, pl.ds(k, 8, stride=m), :] for k in range(m)] for h in range(2)]


def store_rows(ref, state, first=0):
    m = len(state[0])
    for h in range(2):
        for k in range(m):
            ref[h, pl.ds(first + k, 8, stride=m), :] = state[h][k]


def load_state(ref):
    return [[ref[h, k] for k in range(ref.shape[1])] for h in range(2)]


def store_state(ref, state):
    for h in range(2):
        for k in range(len(state[h])):
            ref[h, k] = state[h][k]


def plus(state, addend):
    return [[x + y for x, y in zip(s, t)] for s, t in zip(state, addend)]


def minus(state, addend):
    return [[x - y for x, y in zip(s, t)] for s, t in zip(state, addend)]


def repeat(state, a_ref, b_ref, scale, count, unroll):
    def turn(_, carried):
        carried = [list(half) for half in carried]
        for _ in range(unroll):
            carried = advance(carried, a_ref, b_ref, scale)
        return tuple(tuple(half) for half in carried)

    state = tuple(tuple(half) for half in state)
    state = lax.fori_loop(0, count // unroll, turn, state)
    return [list(half) for half in state]


def widen(ext, values):
    for h in range(2):
        part = values[:, h * LANES : (h + 1) * LANES]
        ext[h, HALO : HALO + N] = part
        ext[h, 0:HALO] = part[N - HALO :]
        ext[h, HALO + N :] = part[:HALO]


def copy_strip(dst, ext, first):
    for h in range(2):
        for row in range(0, ROWS, 8):
            src = pl.ds(pl.multiple_of(first + row, 8), 8)
            dst[h, row : row + 8] = ext[h, src]


def kernel(
    init_ref,
    rate_ref,
    guess_ref,
    points_ref,
    corner_ref,
    init_in,
    rate_in,
    prior_in,
    perm,
    init_ext,
    rate_ext,
    relaxed_ext,
    strip,
    a_full,
    b_full,
    a_1,
    b_1,
    a_16,
    b_16,
    a_64,
    b_64,
    starts,
    terms,
    corner_rows,
    corner_full,
    fresh,
    ct_rows,
    ct,
    cts,
    history,
    hop_rows,
    z_stage,
    pass_rows,
    z_in,
    z_own,
    point_rows,
    points_full,
    in_sem,
    start_send,
    start_recv,
    forward_send,
    corner_send,
    corner_recv,
    fresh_send,
    fresh_recv,
    ct_send,
    ct_recv,
    hop_send,
    hop_recv,
    pass_send,
    pass_recv,
    point_send,
    point_recv,
):
    group = lax.axis_index("tm")
    member = lax.axis_index("grp")
    groups = 32
    x, y, c = group // 8, (group // 2) % 4, group % 2
    stage = x // 2
    chip_x = x % 2
    local_group = group % STAGE
    core0 = c == 0

    def around(distance):
        return (member + distance) % 4

    first = jnp.logical_and(group == 0, member == 0)
    rate_copy = pltpu.make_async_copy(rate_ref, rate_in, in_sem.at[0])
    rate_copy.start()
    prior_copies = (
        pltpu.make_async_copy(init_ref, prior_in, in_sem.at[1]),
        pltpu.make_async_copy(guess_ref.at[0], prior_in, in_sem.at[1]),
    )
    pl.when(first)(prior_copies[0].start)
    pl.when(jnp.logical_not(first))(prior_copies[1].start)
    init_copy = pltpu.make_async_copy(init_ref, init_in, in_sem.at[2])
    init_copy.start()

    barrier = pltpu.get_barrier_semaphore()

    def greet(tm, grp):
        pl.semaphore_signal(barrier, inc=1, device_id=(tm, grp), device_id_type=MESH)

    for d in (1, 2, 3):
        greet(group, around(d))

    @pl.when(group > 0)
    def _():
        greet(group - 1, 3)
        greet(group - 1, member)

    @pl.when(core0)
    def _():
        for dx in range(2):
            for dy in range(4):
                px, py = stage * 2 + (chip_x + dx) % 2, (y + dy) % 4
                if (dx, dy) != (0, 0):
                    greet(at_xy(px, py, 0), member)
                greet(at_xy(px, py, 1), member)

    @pl.when(jnp.logical_and(core0, stage == 1))
    def _():
        for d in (0, 1, 3):
            greet(at_xy(3 - x, y, 0), around(d))

    @pl.when(c == 1)
    def _():
        greet(group - 1, member)

    more = (group < groups - 1).astype(jnp.int32)
    expected = (
        3
        + more * (1 + 4 * (member == 3).astype(jnp.int32))
        + 7
        + c
        + (1 - c) * (1 + 3 * (1 - stage))
    )

    perm[...] = permutation(False)
    rate_copy.wait()
    rate = permuted(rate_in[...], perm[...])
    widen(rate_ext, rate)
    prior_copies[1].wait()
    prior = permuted(prior_in[...], perm[...])
    for h in range(2):
        relaxed_ext[h, HALO : HALO + N] = prior[:, h * LANES : (h + 1) * LANES]
    full = relaxed_ext.at[:, HALO : HALO + N]
    rates = load_rows(rate_ext.at[:, HALO : HALO + N], MF)
    for h in range(2):
        for k in range(MF):
            a_full[h, k] = (1.0 - 4.0 * KAPPA) + rates[h][k]
            b_full[h, k] = rates[h][k]
    relaxed = repeat(load_rows(full, MF), a_full, b_full, KAPPA, STEPS, 8)
    store_rows(relaxed_ext, relaxed, HALO)
    for h in range(2):
        relaxed_ext[h, 0:HALO] = relaxed_ext[h, N : N + HALO]
        relaxed_ext[h, HALO + N :] = relaxed_ext[h, HALO : 2 * HALO]

    pl.semaphore_wait(barrier, expected)

    pending = []
    slot = (member + 1) % 4
    target = group + (member == 3).astype(jnp.int32)
    have = jnp.logical_or(member < 3, group < groups - 1)
    for d, part, low, high in (
        (1, 0, CORE, ROWS),
        (3, 0, 0, ROWS - CORE),
        (1, 1, 0, CORE),
        (3, 1, ROWS - CORE, ROWS),
        (0, 0, 0, ROWS),
    ):
        q = around(d)
        copy = pltpu.make_async_remote_copy(
            src_ref=relaxed_ext.at[
                :, pl.ds(pl.multiple_of(q * CORE + low, 8), high - low)
            ],
            dst_ref=starts.at[slot, :, low:high],
            send_sem=start_send.at[2 * d + part if d else 0],
            recv_sem=start_recv.at[slot, part],
            device_id=(target, q),
            device_id_type=MESH,
        )
        when = have if d else jnp.logical_and(have, member == 3)
        pl.when(when)(copy.start)
        pending.append((when, copy))

    own_first = pl.multiple_of(member * CORE, 8)

    @pl.when(member < 3)
    def _():
        copy_strip(starts.at[slot], relaxed_ext, own_first)

    init_copy.wait()
    widen(init_ext, permuted(init_in[...], perm[...]))

    @pl.when(group == 0)
    def _():
        copy_strip(starts.at[0], init_ext, own_first)
        copy_strip(fresh, init_ext, own_first)

    copy_strip(strip, rate_ext, own_first)
    rates = load_rows(strip, M)
    for h in range(2):
        for k in range(M):
            r = rates[h][k]
            for factor, a_ref, b_ref in (
                (1.0, a_1, b_1),
                (16.0, a_16, b_16),
                (64.0, a_64, b_64),
            ):
                a_ref[h, k] = (1.0 - 4.0 * KAPPA * factor) + factor * r
                b_ref[h, k] = factor * r
    copy_strip(strip, init_ext, own_first)
    perm[...] = permutation(True)

    def arrived(s, low, high, part):
        pltpu.make_async_remote_copy(
            src_ref=starts.at[s, :, low:high],
            dst_ref=starts.at[s, :, low:high],
            send_sem=start_send.at[0],
            recv_sem=start_recv.at[s, part],
            device_id=(group, around(1)),
            device_id_type=MESH,
        ).wait_recv()

    def make_terms(slots):
        for s in slots:
            start = load_rows(starts.at[s], M)
            store_state(terms.at[s], advance(start, a_16, b_16, 16.0 * KAPPA))

        def turn(_, carried):
            for _ in range(8):
                carried = [advance(state, a_1, b_1, KAPPA) for state in carried]
            return tuple(tuple(tuple(half) for half in state) for state in carried)

        carried = tuple(
            tuple(tuple(half) for half in load_rows(starts.at[s], M)) for s in slots
        )
        fine = lax.fori_loop(0, STEPS // 8, turn, carried)
        for s, state in zip(slots, fine):
            store_state(terms.at[s], minus(state, load_state(terms.at[s])))

    below, above, far = (slot + 3) % 4, (slot + 1) % 4, (slot + 2) % 4

    def there(s):
        return jnp.logical_or(s != 0, group > 0)

    @pl.when(member < 3)
    def _():
        make_terms([slot])

    half = ROWS // 2
    for s, part, low, to, to_low, d in (
        (below, 0, CORE, 0, 0, 1),
        (above, 0, 8, 1, half, 3),
    ):
        copy = pltpu.make_async_remote_copy(
            src_ref=starts.at[s, :, low : low + half],
            dst_ref=starts.at[s, :, to_low : to_low + half],
            send_sem=forward_send.at[to],
            recv_sem=start_recv.at[s, to],
            device_id=(group, around(d)),
            device_id_type=MESH,
        )

        @pl.when(there(s))
        def _(s=s, d=d, copy=copy):
            arrived(s, *((CORE, ROWS) if d == 1 else (0, ROWS - CORE)), 0)
            copy.start()

        pending.append((there(s), copy))

    @pl.when(member == 3)
    def _():
        @pl.when(group > 0)
        def _():
            arrived(slot, 0, ROWS, 0)

        make_terms([slot])

    @pl.when(there(below))
    def _():
        arrived(below, 0, CORE, 1)

    @pl.when(there(above))
    def _():
        arrived(above, ROWS - CORE, ROWS, 1)

    make_terms([below, above])

    @pl.when(there(far))
    def _():
        arrived(far, 0, half, 0)
        arrived(far, half, ROWS, 1)

    make_terms([far])

    def big_step(state, index):
        stepped = advance(state, a_16, b_16, 16.0 * KAPPA)
        return plus(stepped, load_state(terms.at[index]))

    corner = load_rows(starts.at[0], M)
    for index in range(4):
        corner = big_step(corner, index)
    store_rows(corner_rows, corner)
    sent = slice(HALO - 24, HALO + CORE + 24)
    fresh_copies = []
    for h in range(1):
        copy = pltpu.make_async_remote_copy(
            src_ref=corner_rows.at[:, sent],
            dst_ref=fresh.at[:, sent],
            send_sem=fresh_send.at[h],
            recv_sem=fresh_recv.at[h],
            device_id=(lax.rem(group + 1, groups), member),
            device_id_type=MESH,
        )
        fresh_copies.append(copy)
        pl.when(group < groups - 1)(copy.start)
        pending.append((group < groups - 1, copy))
    core_rows = slice(HALO, HALO + CORE)
    own_rows = pl.ds(own_first, CORE)
    for d in (1, 3, 2):
        copy = pltpu.make_async_remote_copy(
            src_ref=corner_rows.at[:, core_rows],
            dst_ref=corner_full.at[:, own_rows],
            send_sem=corner_send.at[d - 1],
            recv_sem=corner_recv.at[member],
            device_id=(group, around(d)),
            device_id_type=MESH,
        )
        copy.start()
        pending.append((None, copy))
    for h in range(2):
        corner_full[h, own_rows] = corner_rows[h, core_rows]

    for copy in fresh_copies:
        pl.when(group > 0)(copy.wait_recv)
    state = load_rows(fresh, M)
    for index in range(4):
        state = big_step(state, index)
    state = minus(state, advance(load_rows(fresh, M), a_64, b_64, 64.0 * KAPPA))
    store_state(ct, state)
    store_rows(ct_rows, state)
    def ct_copies(halo):
        rows = slice(HALO - halo, HALO + CORE + halo)
        copies = []
        for dx in (1, 0):
            for dy in (2, 1, 3, 0):
                px, py = stage * 2 + (chip_x + dx) % 2, (y + dy) % 4
                copies.append(
                    pltpu.make_async_remote_copy(
                        src_ref=ct_rows.at[:, rows],
                        dst_ref=cts.at[local_group, :, rows],
                        send_sem=ct_send.at[dx * 4 + dy],
                        recv_sem=ct_recv.at[local_group],
                        device_id=(at_xy(px, py, 0), member),
                        device_id_type=MESH,
                    )
                )
        return copies

    widths = (
        (24, local_group == 0),
        (16, jnp.logical_and(local_group > 0, local_group <= 8)),
        (8, local_group > 8),
    )
    for halo, when in widths:

        @pl.when(when)
        def _(halo=halo):
            copies = ct_copies(halo)
            for copy in copies[:-1]:
                copy.start()
            pl.when(c == 1)(copies[-1].start)

    for d in (1, 3, 2):
        q = around(d)
        pltpu.make_async_remote_copy(
            src_ref=corner_rows.at[:, core_rows],
            dst_ref=corner_full.at[:, pl.ds(pl.multiple_of(q * CORE, 8), CORE)],
            send_sem=corner_send.at[0],
            recv_sem=corner_recv.at[q],
            device_id=(group, q),
            device_id_type=MESH,
        ).wait_recv()
    both = jnp.concatenate([corner_full[0], corner_full[1]], axis=1)
    corner_ref[...] = permuted(both, perm[...])

    hop = []
    rows = 24
    for d, src, dst in (
        (3, HALO, HALO + CORE),
        (1, HALO + CORE - rows, HALO - rows),
        (0, HALO, HALO),
    ):
        count = rows if d else CORE
        hop.append(
            pltpu.make_async_remote_copy(
                src_ref=hop_rows.at[:, src : src + count],
                dst_ref=z_stage.at[:, dst : dst + count],
                send_sem=hop_send.at[d],
                recv_sem=hop_recv.at[d],
                device_id=(at_xy(3 - x, y, 0), around(d)),
                device_id_type=MESH,
            )
        )
    handed = slice(HALO - 8, HALO + CORE + 8)
    pass_copy = pltpu.make_async_remote_copy(
        src_ref=pass_rows.at[:, handed],
        dst_ref=z_in.at[:, handed],
        send_sem=pass_send,
        recv_sem=pass_recv,
        device_id=(at_xy(x, y, 1), member),
        device_id_type=MESH,
    )

    @pl.when(core0)
    def _():
        store_rows(cts.at[local_group], load_state(ct))

        @pl.when(stage == 0)
        def _():
            store_state(history.at[0], load_rows(strip, M))

        @pl.when(stage == 1)
        def _():
            for copy in hop:
                copy.wait_recv()
            store_state(history.at[0], load_rows(z_stage, M))

        last = load_state(history.at[0])
        for t in range(STAGE):
            if t % 4 == 0:
                for n in range(t, t + 4):
                    halo = 24 if n == 0 else 16 if n <= 8 else 8
                    rows = slice(HALO - halo, HALO + CORE + halo)

                    @pl.when(n != local_group)
                    def _(n=n, rows=rows):
                        pltpu.make_async_remote_copy(
                            src_ref=ct_rows.at[:, rows],
                            dst_ref=cts.at[n, :, rows],
                            send_sem=ct_send.at[0],
                            recv_sem=ct_recv.at[n],
                            device_id=(group, around(1)),
                            device_id_type=MESH,
                        ).wait_recv()

            last = advance(last, a_64, b_64, 64.0 * KAPPA)
            last = plus(last, load_rows(cts.at[t], M))
            store_state(history.at[t + 1], last)

        @pl.when(stage == 0)
        def _():
            store_rows(hop_rows, last)
            for copy in hop:
                copy.start()

        store_rows(pass_rows, load_state(history.at[local_group + 1]))
        pass_copy.start()
        store_state(z_own, load_state(history.at[local_group]))

    @pl.when(c == 1)
    def _():
        pass_copy.wait_recv()
        store_state(z_own, load_rows(z_in, M))

    final = load_state(z_own)
    final = plus(advance(final, a_64, b_64, 64.0 * KAPPA), load_state(ct))
    state = load_state(z_own)
    for index in (3, 0, 1, 2):
        if index < 3:
            state = big_step(state, index)
        store_rows(point_rows.at[index], state if index < 3 else final)

        copy = pltpu.make_async_remote_copy(
            src_ref=point_rows.at[index, :, core_rows],
            dst_ref=points_full.at[:, own_rows],
            send_sem=point_send.at[index],
            recv_sem=point_recv.at[member],
            device_id=(group, index),
            device_id_type=MESH,
        )
        when = member != index
        pl.when(when)(copy.start)
        pending.append((when, copy))
    for h in range(2):
        points_full[h, own_rows] = point_rows[member, h, core_rows]
    for d in (0, 1, 3, 2):
        q = around(d)
        rows = pl.ds(pl.multiple_of(q * CORE, 8), CORE)
        if d:
            pltpu.make_async_remote_copy(
                src_ref=point_rows.at[0, :, core_rows],
                dst_ref=points_full.at[:, rows],
                send_sem=point_send.at[0],
                recv_sem=point_recv.at[q],
                device_id=(group, q),
                device_id_type=MESH,
            ).wait_recv()
        both = jnp.concatenate([points_full[0, rows], points_full[1, rows]], axis=1)
        points_ref[rows] = permuted(both, perm[...])

    for when, copy in pending:
        if when is None:
            copy.wait_send()
        else:
            pl.when(when)(copy.wait_send)

    for halo, when in widths:

        @pl.when(when)
        def _(halo=halo):
            copies = ct_copies(halo)
            for copy in copies[:-1]:
                copy.wait_send()
            pl.when(c == 1)(copies[-1].wait_send)

    @pl.when(core0)
    def _():
        pass_copy.wait_send()

        @pl.when(stage == 0)
        def _():
            for copy in hop:
                copy.wait_send()


def write_out(points, corner, points_out, corner_out, sems):
    copies = (
        pltpu.make_async_copy(points, points_out.at[0], sems.at[0]),
        pltpu.make_async_copy(corner, corner_out.at[0], sems.at[1]),
    )
    for copy in copies:
        copy.start()
    for copy in copies:
        copy.wait()


def local(init_field, reaction, guesses):
    vmem = pl.BlockSpec(memory_space=pltpu.VMEM)
    strip_state = pltpu.VMEM((2, M, 8, LANES), F32)
    full_state = pltpu.VMEM((2, MF, 8, LANES), F32)
    strip_rows = pltpu.VMEM((2, ROWS, LANES), F32)
    ext_rows = pltpu.VMEM((2, N + 2 * HALO, LANES), F32)
    full_rows = pltpu.VMEM((2, N, LANES), F32)
    dma = pltpu.SemaphoreType.DMA

    def many(count, *shape):
        return pltpu.VMEM((count, *shape), F32)

    scratch = [
        *[pltpu.VMEM((N, N), F32)] * 3,
        pltpu.VMEM((N, N), jnp.bfloat16),
        ext_rows,
        ext_rows,
        ext_rows,
        strip_rows,
        full_state,
        full_state,
        *[strip_state] * 6,
        many(4, 2, ROWS, LANES),
        many(4, 2, M, 8, LANES),
        strip_rows,
        full_rows,
        strip_rows,
        strip_rows,
        strip_state,
        many(STAGE, 2, ROWS, LANES),
        many(STAGE + 1, 2, M, 8, LANES),
        strip_rows,
        strip_rows,
        strip_rows,
        strip_rows,
        strip_state,
        many(4, 2, ROWS, LANES),
        full_rows,
        dma((3,)),
        dma((8,)),
        dma((4, 2)),
        dma((2,)),
        dma((3,)),
        dma((4,)),
        dma((2,)),
        dma((2,)),
        dma((8,)),
        dma((STAGE,)),
        dma((4,)),
        dma((4,)),
        dma,
        dma,
        dma((4,)),
        dma((4,)),
    ]
    hbm = pl.BlockSpec(memory_space=pltpu.HBM)
    points, corner = pl.pallas_call(
        kernel,
        out_shape=(
            jax.ShapeDtypeStruct((N, N), F32),
            jax.ShapeDtypeStruct((N, N), F32),
        ),
        in_specs=[hbm] * 3,
        out_specs=(vmem, vmem),
        scratch_shapes=scratch,
        compiler_params=pltpu.CompilerParams(
            collective_id=0, has_side_effects=True, vmem_limit_bytes=213 * 2**18
        ),
    )(init_field, reaction, guesses)
    block = jax.ShapeDtypeStruct((1, N, N), F32)
    return pl.pallas_call(
        write_out,
        out_shape=(block, block),
        in_specs=[vmem] * 2,
        out_specs=(hbm, hbm),
        scratch_shapes=[dma((2,))],
        compiler_params=pltpu.CompilerParams(vmem_limit_bytes=8 * 2**20),
    )(points, corner)


def solution(mesh):
    return jax.shard_map(
        local,
        mesh=mesh,
        in_specs=(P(), P(), P(("tm", "grp"), None, None)),
        out_specs=(P(("tm", "grp"), None, None), P("tm", None, None)),
        check_vma=False,
    )
```

```python
import functools

import jax
import jax.numpy as jnp
from jax import lax
from jax.experimental import pallas as pl
from jax.experimental.pallas import tpu as pltpu
from jax.sharding import PartitionSpec as P

STEPS = 16
KAPPA = 0.0035
MESH = pl.DeviceIdType.MESH

N = 256
LANES = 128
HALO = 40
CORE = 64
ROWS = CORE + 2 * HALO
M = ROWS // 8
MF = N // 8
STAGE = 16
HALF = CORE // 2
EDGE = 24
HALF_ROWS = HALF + 2 * EDGE
MH = HALF_ROWS // 8
F32 = jnp.float32


def at_xy(x, y, c):
    return (x * 4 + y) * 2 + c


def permutation(transposed):
    big = lax.broadcasted_iota(jnp.int32, (N, N), 1 if transposed else 0)
    new = lax.broadcasted_iota(jnp.int32, (N, N), 0 if transposed else 1)
    wanted = 2 * (new % LANES) + new // LANES
    return (big == wanted).astype(F32).astype(jnp.bfloat16)


def permuted(values, matrix):
    high = values.astype(jnp.bfloat16)
    rest = values - high.astype(F32)
    middle = rest.astype(jnp.bfloat16)
    low = (rest - middle.astype(F32)).astype(jnp.bfloat16)
    dot = functools.partial(jnp.dot, preferred_element_type=F32)
    return (dot(high, matrix) + dot(middle, matrix)) + dot(low, matrix)


def advance(state, a_ref, b_ref, scale):
    left, right = state
    m = len(left)
    new_left, new_right = [], []
    for k in range(m):
        u, v = left[k], right[k]
        above = [
            pltpu.roll(half[m - 1], 1, 0) if k == 0 else half[k - 1] for half in state
        ]
        below = [
            pltpu.roll(half[0], 7, 0) if k == m - 1 else half[k + 1] for half in state
        ]
        su = above[0] + below[0] + (v + pltpu.roll(v, 1, 1))
        sv = above[1] + below[1] + (u + pltpu.roll(u, LANES - 1, 1))
        new_left.append(scale * su + u * (a_ref[0, k] - b_ref[0, k] * (u * u)))
        new_right.append(scale * sv + v * (a_ref[1, k] - b_ref[1, k] * (v * v)))
    return new_left, new_right


def load_rows(ref, m):
    return [[ref[h, pl.ds(k, 8, stride=m), :] for k in range(m)] for h in range(2)]


def store_rows(ref, state, first=0):
    m = len(state[0])
    for h in range(2):
        for k in range(m):
            ref[h, pl.ds(first + k, 8, stride=m), :] = state[h][k]


def load_state(ref):
    return [[ref[h, k] for k in range(ref.shape[1])] for h in range(2)]


def store_state(ref, state):
    for h in range(2):
        for k in range(len(state[h])):
            ref[h, k] = state[h][k]


def plus(state, addend):
    return [[x + y for x, y in zip(s, t)] for s, t in zip(state, addend)]


def minus(state, addend):
    return [[x - y for x, y in zip(s, t)] for s, t in zip(state, addend)]


def repeat(state, a_ref, b_ref, scale, count, unroll):
    def turn(_, carried):
        carried = [list(half) for half in carried]
        for _ in range(unroll):
            carried = advance(carried, a_ref, b_ref, scale)
        return tuple(tuple(half) for half in carried)

    state = tuple(tuple(half) for half in state)
    state = lax.fori_loop(0, count // unroll, turn, state)
    return [list(half) for half in state]


def widen(ext, values):
    for h in range(2):
        part = values[:, h * LANES : (h + 1) * LANES]
        ext[h, HALO : HALO + N] = part
        ext[h, 0:HALO] = part[N - HALO :]
        ext[h, HALO + N :] = part[:HALO]


def copy_strip(dst, ext, first, rows=ROWS):
    for h in range(2):
        for row in range(0, rows, 8):
            src = pl.ds(pl.multiple_of(first + row, 8), 8)
            dst[h, row : row + 8] = ext[h, src]


def kernel(
    init_ref,
    rate_ref,
    guess_ref,
    points_ref,
    corner_ref,
    init_in,
    rate_in,
    prior_in,
    perm,
    init_ext,
    rate_ext,
    relaxed_ext,
    strip,
    a_full,
    b_full,
    a_1,
    b_1,
    a_16,
    b_16,
    a_64,
    b_64,
    starts,
    terms,
    corner_rows,
    corner_full,
    fresh,
    ct_rows,
    ct,
    cts,
    history,
    half_history,
    half_strip,
    a_half,
    b_half,
    hop_rows,
    z_stage,
    pass_rows,
    z_in,
    z_own,
    point_rows,
    points_full,
    in_sem,
    start_send,
    start_recv,
    forward_send,
    corner_send,
    corner_recv,
    fresh_send,
    fresh_recv,
    ct_send,
    ct_recv,
    hop_send,
    hop_recv,
    pass_send,
    pass_recv,
    point_send,
    point_recv,
):
    group = lax.axis_index("tm")
    member = lax.axis_index("grp")
    groups = 32
    x, y, c = group // 8, (group // 2) % 4, group % 2
    stage = x // 2
    chip_x = x % 2
    local_group = group % STAGE
    core0 = c == 0
    mine = (x + y) % 2
    half_first = HALO - EDGE + HALF * mine

    def around(distance):
        return (member + distance) % 4

    first = jnp.logical_and(group == 0, member == 0)
    rate_copy = pltpu.make_async_copy(rate_ref, rate_in, in_sem.at[0])
    rate_copy.start()
    prior_copies = (
        pltpu.make_async_copy(init_ref, prior_in, in_sem.at[1]),
        pltpu.make_async_copy(guess_ref.at[0], prior_in, in_sem.at[1]),
    )
    pl.when(first)(prior_copies[0].start)
    pl.when(jnp.logical_not(first))(prior_copies[1].start)
    init_copy = pltpu.make_async_copy(init_ref, init_in, in_sem.at[2])
    init_copy.start()

    barrier = pltpu.get_barrier_semaphore()

    def greet(tm, grp):
        pl.semaphore_signal(barrier, inc=1, device_id=(tm, grp), device_id_type=MESH)

    for d in (1, 2, 3):
        greet(group, around(d))

    @pl.when(group > 0)
    def _():
        greet(group - 1, 3)
        greet(group - 1, member)

    @pl.when(core0)
    def _():
        for dx in range(2):
            for dy in range(4):
                px, py = stage * 2 + (chip_x + dx) % 2, (y + dy) % 4
                if (dx, dy) != (0, 0):
                    greet(at_xy(px, py, 0), member)
                greet(at_xy(px, py, 1), member)

    @pl.when(jnp.logical_and(core0, stage == 1))
    def _():
        for dy in (0, 3):
            py = (y + dy) % 4
            greet(at_xy(3 - x, py, 0), member)
            greet(at_xy(3 - x, py, 0), around(1 + 2 * ((3 - x + py) % 2)))

    @pl.when(c == 1)
    def _():
        greet(group - 1, member)

    @pl.when(stage == 0)
    def _():
        greet(at_xy(1 - x, y, 0), member)

    more = (group < groups - 1).astype(jnp.int32)
    expected = (
        3
        + more * (1 + 4 * (member == 3).astype(jnp.int32))
        + 7
        + c
        + (1 - c) * (1 + 6 * (1 - stage))
    )

    perm[...] = permutation(False)
    rate_copy.wait()
    rate = permuted(rate_in[...], perm[...])
    widen(rate_ext, rate)
    prior_copies[1].wait()
    prior = permuted(prior_in[...], perm[...])
    for h in range(2):
        relaxed_ext[h, HALO : HALO + N] = prior[:, h * LANES : (h + 1) * LANES]
    full = relaxed_ext.at[:, HALO : HALO + N]
    rates = load_rows(rate_ext.at[:, HALO : HALO + N], MF)
    for h in range(2):
        for k in range(MF):
            a_full[h, k] = (1.0 - 4.0 * KAPPA) + rates[h][k]
            b_full[h, k] = rates[h][k]
    relaxed = repeat(load_rows(full, MF), a_full, b_full, KAPPA, STEPS, 8)
    store_rows(relaxed_ext, relaxed, HALO)
    for h in range(2):
        relaxed_ext[h, 0:HALO] = relaxed_ext[h, N : N + HALO]
        relaxed_ext[h, HALO + N :] = relaxed_ext[h, HALO : 2 * HALO]

    pl.semaphore_wait(barrier, expected)

    pending = []
    slot = (member + 1) % 4
    target = group + (member == 3).astype(jnp.int32)
    have = jnp.logical_or(member < 3, group < groups - 1)
    for d, part, low, high in (
        (1, 0, CORE, ROWS),
        (3, 0, 0, ROWS - CORE),
        (1, 1, 0, CORE),
        (3, 1, ROWS - CORE, ROWS),
        (0, 0, 0, ROWS),
    ):
        q = around(d)
        copy = pltpu.make_async_remote_copy(
            src_ref=relaxed_ext.at[
                :, pl.ds(pl.multiple_of(q * CORE + low, 8), high - low)
            ],
            dst_ref=starts.at[slot, :, low:high],
            send_sem=start_send.at[2 * d + part if d else 0],
            recv_sem=start_recv.at[slot, part],
            device_id=(target, q),
            device_id_type=MESH,
        )
        when = have if d else jnp.logical_and(have, member == 3)
        pl.when(when)(copy.start)
        pending.append((when, copy))

    own_first = pl.multiple_of(member * CORE, 8)

    @pl.when(member < 3)
    def _():
        copy_strip(starts.at[slot], relaxed_ext, own_first)

    init_copy.wait()
    widen(init_ext, permuted(init_in[...], perm[...]))

    @pl.when(group == 0)
    def _():
        copy_strip(starts.at[0], init_ext, own_first)
        copy_strip(fresh, init_ext, own_first)

    copy_strip(strip, rate_ext, own_first)
    rates = load_rows(strip, M)
    for h in range(2):
        for k in range(M):
            r = rates[h][k]
            for factor, a_ref, b_ref in (
                (1.0, a_1, b_1),
                (16.0, a_16, b_16),
                (64.0, a_64, b_64),
            ):
                a_ref[h, k] = (1.0 - 4.0 * KAPPA * factor) + factor * r
                b_ref[h, k] = factor * r
    copy_strip(strip, init_ext, own_first)
    perm[...] = permutation(True)

    @pl.when(jnp.logical_and(core0, stage == 0))
    def _():
        first_row = own_first + half_first
        copy_strip(half_strip, rate_ext, first_row, HALF_ROWS)
        rates = load_rows(half_strip, MH)
        for h in range(2):
            for k in range(MH):
                r = 64.0 * rates[h][k]
                a_half[h, k] = (1.0 - 4.0 * KAPPA * 64.0) + r
                b_half[h, k] = r
        copy_strip(half_strip, init_ext, first_row, HALF_ROWS)

    def arrived(s, low, high, part):
        pltpu.make_async_remote_copy(
            src_ref=starts.at[s, :, low:high],
            dst_ref=starts.at[s, :, low:high],
            send_sem=start_send.at[0],
            recv_sem=start_recv.at[s, part],
            device_id=(group, around(1)),
            device_id_type=MESH,
        ).wait_recv()

    def make_terms(slots):
        for s in slots:
            start = load_rows(starts.at[s], M)
            store_state(terms.at[s], advance(start, a_16, b_16, 16.0 * KAPPA))

        def turn(_, carried):
            for _ in range(8):
                carried = [advance(state, a_1, b_1, KAPPA) for state in carried]
            return tuple(tuple(tuple(half) for half in state) for state in carried)

        carried = tuple(
            tuple(tuple(half) for half in load_rows(starts.at[s], M)) for s in slots
        )
        fine = lax.fori_loop(0, STEPS // 8, turn, carried)
        for s, state in zip(slots, fine):
            store_state(terms.at[s], minus(state, load_state(terms.at[s])))

    below, above, far = (slot + 3) % 4, (slot + 1) % 4, (slot + 2) % 4

    def there(s):
        return jnp.logical_or(s != 0, group > 0)

    @pl.when(member < 3)
    def _():
        make_terms([slot])

    half = ROWS // 2
    for s, part, low, to, to_low, d in (
        (below, 0, CORE, 0, 0, 1),
        (above, 0, 8, 1, half, 3),
    ):
        copy = pltpu.make_async_remote_copy(
            src_ref=starts.at[s, :, low : low + half],
            dst_ref=starts.at[s, :, to_low : to_low + half],
            send_sem=forward_send.at[to],
            recv_sem=start_recv.at[s, to],
            device_id=(group, around(d)),
            device_id_type=MESH,
        )

        @pl.when(there(s))
        def _(s=s, d=d, copy=copy):
            arrived(s, *((CORE, ROWS) if d == 1 else (0, ROWS - CORE)), 0)
            copy.start()

        pending.append((there(s), copy))

    @pl.when(member == 3)
    def _():
        @pl.when(group > 0)
        def _():
            arrived(slot, 0, ROWS, 0)

        make_terms([slot])

    @pl.when(there(below))
    def _():
        arrived(below, 0, CORE, 1)

    @pl.when(there(above))
    def _():
        arrived(above, ROWS - CORE, ROWS, 1)

    make_terms([below, above])

    @pl.when(there(far))
    def _():
        arrived(far, 0, half, 0)
        arrived(far, half, ROWS, 1)

    make_terms([far])

    def big_step(state, index):
        stepped = advance(state, a_16, b_16, 16.0 * KAPPA)
        return plus(stepped, load_state(terms.at[index]))

    corner = load_rows(starts.at[0], M)
    for index in range(4):
        corner = big_step(corner, index)
    store_rows(corner_rows, corner)
    sent = slice(HALO - 24, HALO + CORE + 24)
    fresh_copies = []
    for h in range(1):
        copy = pltpu.make_async_remote_copy(
            src_ref=corner_rows.at[:, sent],
            dst_ref=fresh.at[:, sent],
            send_sem=fresh_send.at[h],
            recv_sem=fresh_recv.at[h],
            device_id=(lax.rem(group + 1, groups), member),
            device_id_type=MESH,
        )
        fresh_copies.append(copy)
        pl.when(group < groups - 1)(copy.start)
        pending.append((group < groups - 1, copy))
    core_rows = slice(HALO, HALO + CORE)
    own_rows = pl.ds(own_first, CORE)
    for d in (1, 3, 2):
        copy = pltpu.make_async_remote_copy(
            src_ref=corner_rows.at[:, core_rows],
            dst_ref=corner_full.at[:, own_rows],
            send_sem=corner_send.at[d - 1],
            recv_sem=corner_recv.at[member],
            device_id=(group, around(d)),
            device_id_type=MESH,
        )
        copy.start()
        pending.append((None, copy))
    for h in range(2):
        corner_full[h, own_rows] = corner_rows[h, core_rows]

    for copy in fresh_copies:
        pl.when(group > 0)(copy.wait_recv)
    state = load_rows(fresh, M)
    for index in range(4):
        state = big_step(state, index)
    state = minus(state, advance(load_rows(fresh, M), a_64, b_64, 64.0 * KAPPA))
    store_state(ct, state)
    store_rows(ct_rows, state)
    def ct_copies(halo, of_stage):
        copies = []
        for dx in (1, 0):
            for dy in (2, 1, 3, 0):
                px, py = of_stage * 2 + (chip_x + dx) % 2, (y + dy) % 4
                if of_stage:
                    src = dst = slice(HALO - halo, HALO + CORE + halo)
                else:
                    its_first = HALO - halo + HALF * ((px + py) % 2)
                    src = pl.ds(pl.multiple_of(its_first, 8), HALF + 2 * halo)
                    dst = slice(EDGE - halo, EDGE + HALF + halo)
                copies.append(
                    pltpu.make_async_remote_copy(
                        src_ref=ct_rows.at[:, src],
                        dst_ref=cts.at[local_group, :, dst],
                        send_sem=ct_send.at[dx * 4 + dy],
                        recv_sem=ct_recv.at[local_group],
                        device_id=(at_xy(px, py, 0), member),
                        device_id_type=MESH,
                    )
                )
        return copies

    widths = (
        (24, local_group == 0),
        (16, jnp.logical_and(local_group > 0, local_group <= 8)),
        (8, local_group > 8),
    )
    for halo, when in widths:
        for of_stage in range(2):

            @pl.when(jnp.logical_and(when, stage == of_stage))
            def _(halo=halo, of_stage=of_stage):
                copies = ct_copies(halo, of_stage)
                for copy in copies[:-1]:
                    copy.start()
                pl.when(c == 1)(copies[-1].start)

    for d in (1, 3, 2):
        q = around(d)
        pltpu.make_async_remote_copy(
            src_ref=corner_rows.at[:, core_rows],
            dst_ref=corner_full.at[:, pl.ds(pl.multiple_of(q * CORE, 8), CORE)],
            send_sem=corner_send.at[0],
            recv_sem=corner_recv.at[q],
            device_id=(group, q),
            device_id_type=MESH,
        ).wait_recv()
    both = jnp.concatenate([corner_full[0], corner_full[1]], axis=1)
    corner_ref[...] = permuted(both, perm[...])

    def remote(src, dst, send, recv, tm, grp=member):
        return pltpu.make_async_remote_copy(
            src_ref=src,
            dst_ref=dst,
            send_sem=send,
            recv_sem=recv,
            device_id=(tm, grp),
            device_id_type=MESH,
        )

    def rows_at(first, count):
        return pl.ds(pl.multiple_of(first, 8), count)

    hop = []
    for dy in (1, 0):
        tm = at_xy(3 - x, (y + dy) % 4, 0)
        hop.append(
            remote(
                hop_rows.at[:, rows_at(EDGE + 8 * mine, EDGE)],
                z_stage.at[:, rows_at(HALO + CORE - (CORE + EDGE) * mine, EDGE)],
                hop_send.at[2 * dy],
                hop_recv.at[2 + mine],
                tm,
                around(3 - 2 * mine),
            )
        )
        hop.append(
            remote(
                hop_rows.at[:, EDGE : EDGE + HALF],
                z_stage.at[:, rows_at(HALO + HALF * mine, HALF)],
                hop_send.at[2 * dy + 1],
                hop_recv.at[mine],
                tm,
            )
        )
    hop_arrivals = []
    for n, (first, count) in enumerate(
        (
            (HALO, HALF),
            (HALO + HALF, HALF),
            (HALO + CORE, EDGE),
            (HALO - EDGE, EDGE),
        )
    ):
        there_rows = z_stage.at[:, first : first + count]
        hop_arrivals.append(
            remote(there_rows, there_rows, hop_send.at[0], hop_recv.at[n], group)
        )

    handed = slice(HALO - 8, HALO + CORE + 8)
    sibling = at_xy(x, y, 1)
    pass_copy = remote(
        pass_rows.at[0, :, handed],
        z_in.at[:, handed],
        pass_send.at[0],
        pass_recv.at[0],
        sibling,
    )
    part = HALF + 8
    half_src, half_dst = 16 + 8 * mine, HALO - 8 + part * mine
    given = []
    for n, tm in enumerate((sibling, at_xy(1 - x, y, 0), at_xy(1 - x, y, 1))):
        given.append(
            remote(
                pass_rows.at[n, :, rows_at(half_src, part)],
                z_in.at[:, rows_at(half_dst, part)],
                pass_send.at[n],
                pass_recv.at[mine],
                tm,
            )
        )

    def half_arrived(which):
        there_rows = z_in.at[:, rows_at(HALO - 8 + part * which, part)]
        remote(
            there_rows, there_rows, pass_send.at[0], pass_recv.at[which], group
        ).wait_recv()

    def chain(begin, a_ref, b_ref, core, states, edge):
        last = begin
        m = len(begin[0])
        for t in range(STAGE):
            if t % 4 == 0:
                for n in range(t, t + 4):
                    halo = 24 if n == 0 else 16 if n <= 8 else 8
                    rows = cts.at[n, :, edge - halo : edge + core + halo]

                    @pl.when(n != local_group)
                    def _(n=n, rows=rows):
                        remote(
                            rows, rows, ct_send.at[0], ct_recv.at[n], sibling
                        ).wait_recv()

            last = advance(last, a_ref, b_ref, 64.0 * KAPPA)
            last = plus(last, load_rows(cts.at[t, :, 0 : 8 * m], m))
            store_state(states.at[t + 1], last)
        return last

    @pl.when(jnp.logical_and(core0, stage == 0))
    def _():
        copy_strip(cts.at[local_group], ct_rows.at[:, :], half_first, HALF_ROWS)
        begin = load_rows(half_strip, MH)
        store_state(half_history.at[0], begin)
        last = chain(begin, a_half, b_half, HALF, half_history, EDGE)
        store_rows(hop_rows, last)
        for copy in hop:
            copy.start()
        other = (local_group + STAGE // 2) % STAGE
        for n, t in enumerate((local_group + 1, other, other + 1)):
            store_rows(pass_rows.at[n], load_state(half_history.at[t]))
            given[n].start()
        store_rows(half_strip, load_state(half_history.at[local_group]))
        for h in range(2):
            z_in[h, rows_at(half_dst, part)] = half_strip[h, rows_at(half_src, part)]

    @pl.when(jnp.logical_and(core0, stage == 1))
    def _():
        store_rows(cts.at[local_group], load_state(ct))
        for copy in hop_arrivals:
            copy.wait_recv()
        begin = load_rows(z_stage, M)
        store_state(history.at[0], begin)
        chain(begin, a_64, b_64, CORE, history, HALO)
        store_rows(pass_rows.at[0], load_state(history.at[local_group + 1]))
        pass_copy.start()
        store_state(z_own, load_state(history.at[local_group]))

    @pl.when(stage == 0)
    def _():
        half_arrived(1 - mine)
        pl.when(c == 1)(lambda: half_arrived(mine))
        store_state(z_own, load_rows(z_in, M))

    @pl.when(jnp.logical_and(c == 1, stage == 1))
    def _():
        pass_copy.wait_recv()
        store_state(z_own, load_rows(z_in, M))

    final = load_state(z_own)
    final = plus(advance(final, a_64, b_64, 64.0 * KAPPA), load_state(ct))
    state = load_state(z_own)
    for index in (3, 0, 1, 2):
        if index < 3:
            state = big_step(state, index)
        store_rows(point_rows.at[index], state if index < 3 else final)

        copy = pltpu.make_async_remote_copy(
            src_ref=point_rows.at[index, :, core_rows],
            dst_ref=points_full.at[:, own_rows],
            send_sem=point_send.at[index],
            recv_sem=point_recv.at[member],
            device_id=(group, index),
            device_id_type=MESH,
        )
        when = member != index
        pl.when(when)(copy.start)
        pending.append((when, copy))
    for h in range(2):
        points_full[h, own_rows] = point_rows[member, h, core_rows]
    for d in (0, 1, 3, 2):
        q = around(d)
        rows = pl.ds(pl.multiple_of(q * CORE, 8), CORE)
        if d:
            pltpu.make_async_remote_copy(
                src_ref=point_rows.at[0, :, core_rows],
                dst_ref=points_full.at[:, rows],
                send_sem=point_send.at[0],
                recv_sem=point_recv.at[q],
                device_id=(group, q),
                device_id_type=MESH,
            ).wait_recv()
        both = jnp.concatenate([points_full[0, rows], points_full[1, rows]], axis=1)
        points_ref[rows] = permuted(both, perm[...])

    for when, copy in pending:
        if when is None:
            copy.wait_send()
        else:
            pl.when(when)(copy.wait_send)

    for halo, when in widths:
        for of_stage in range(2):

            @pl.when(jnp.logical_and(when, stage == of_stage))
            def _(halo=halo, of_stage=of_stage):
                copies = ct_copies(halo, of_stage)
                for copy in copies[:-1]:
                    copy.wait_send()
                pl.when(c == 1)(copies[-1].wait_send)

    @pl.when(jnp.logical_and(core0, stage == 0))
    def _():
        for copy in hop + given:
            copy.wait_send()

    @pl.when(jnp.logical_and(core0, stage == 1))
    def _():
        pass_copy.wait_send()


def write_out(points, corner, points_out, corner_out, sems):
    copies = (
        pltpu.make_async_copy(points, points_out.at[0], sems.at[0]),
        pltpu.make_async_copy(corner, corner_out.at[0], sems.at[1]),
    )
    for copy in copies:
        copy.start()
    for copy in copies:
        copy.wait()


def local(init_field, reaction, guesses):
    vmem = pl.BlockSpec(memory_space=pltpu.VMEM)
    strip_state = pltpu.VMEM((2, M, 8, LANES), F32)
    full_state = pltpu.VMEM((2, MF, 8, LANES), F32)
    strip_rows = pltpu.VMEM((2, ROWS, LANES), F32)
    ext_rows = pltpu.VMEM((2, N + 2 * HALO, LANES), F32)
    full_rows = pltpu.VMEM((2, N, LANES), F32)
    dma = pltpu.SemaphoreType.DMA

    def many(count, *shape):
        return pltpu.VMEM((count, *shape), F32)

    scratch = [
        *[pltpu.VMEM((N, N), F32)] * 3,
        pltpu.VMEM((N, N), jnp.bfloat16),
        ext_rows,
        ext_rows,
        ext_rows,
        strip_rows,
        full_state,
        full_state,
        *[strip_state] * 6,
        many(4, 2, ROWS, LANES),
        many(4, 2, M, 8, LANES),
        strip_rows,
        full_rows,
        strip_rows,
        strip_rows,
        strip_state,
        many(STAGE, 2, ROWS, LANES),
        many(STAGE + 1, 2, M, 8, LANES),
        many(STAGE + 1, 2, MH, 8, LANES),
        pltpu.VMEM((2, HALF_ROWS, LANES), F32),
        *[pltpu.VMEM((2, MH, 8, LANES), F32)] * 2,
        pltpu.VMEM((2, HALF_ROWS, LANES), F32),
        strip_rows,
        many(3, 2, ROWS, LANES),
        strip_rows,
        strip_state,
        many(4, 2, ROWS, LANES),
        full_rows,
        dma((3,)),
        dma((8,)),
        dma((4, 2)),
        dma((2,)),
        dma((3,)),
        dma((4,)),
        dma((2,)),
        dma((2,)),
        dma((8,)),
        dma((STAGE,)),
        dma((4,)),
        dma((4,)),
        dma((3,)),
        dma((2,)),
        dma((4,)),
        dma((4,)),
    ]
    hbm = pl.BlockSpec(memory_space=pltpu.HBM)
    points, corner = pl.pallas_call(
        kernel,
        out_shape=(
            jax.ShapeDtypeStruct((N, N), F32),
            jax.ShapeDtypeStruct((N, N), F32),
        ),
        in_specs=[hbm] * 3,
        out_specs=(vmem, vmem),
        scratch_shapes=scratch,
        compiler_params=pltpu.CompilerParams(
            collective_id=0, has_side_effects=True, vmem_limit_bytes=213 * 2**18
        ),
    )(init_field, reaction, guesses)
    block = jax.ShapeDtypeStruct((1, N, N), F32)
    return pl.pallas_call(
        write_out,
        out_shape=(block, block),
        in_specs=[vmem] * 2,
        out_specs=(hbm, hbm),
        scratch_shapes=[dma((2,))],
        compiler_params=pltpu.CompilerParams(vmem_limit_bytes=8 * 2**20),
    )(points, corner)


def solution(mesh):
    return jax.shard_map(
        local,
        mesh=mesh,
        in_specs=(P(), P(), P(("tm", "grp"), None, None)),
        out_specs=(P(("tm", "grp"), None, None), P("tm", None, None)),
        check_vma=False,
    )
```

```python
import functools

import jax
import jax.numpy as jnp
from jax import lax
from jax.experimental import pallas as pl
from jax.experimental.pallas import tpu as pltpu
from jax.sharding import PartitionSpec as P

STEPS = 16
KAPPA = 0.0035
MESH = pl.DeviceIdType.MESH

N = 256
LANES = 128
HALO = 40
CORE = 64
ROWS = CORE + 2 * HALO
M = ROWS // 8
MF = N // 8
STAGE = 16
HALF = CORE // 2
EDGE = 24
HALF_ROWS = HALF + 2 * EDGE
MH = HALF_ROWS // 8
F32 = jnp.float32


def at_xy(x, y, c):
    return (x * 4 + y) * 2 + c


def permutation(transposed):
    big = lax.broadcasted_iota(jnp.int32, (N, N), 1 if transposed else 0)
    new = lax.broadcasted_iota(jnp.int32, (N, N), 0 if transposed else 1)
    wanted = 2 * (new % LANES) + new // LANES
    return (big == wanted).astype(F32).astype(jnp.bfloat16)


def permuted(values, matrix):
    high = values.astype(jnp.bfloat16)
    rest = values - high.astype(F32)
    middle = rest.astype(jnp.bfloat16)
    low = (rest - middle.astype(F32)).astype(jnp.bfloat16)
    parts = jnp.concatenate([high, middle, low], axis=0)
    moved = jnp.dot(parts, matrix, preferred_element_type=F32)
    rows = values.shape[0]
    return (moved[:rows] + moved[rows : 2 * rows]) + moved[2 * rows :]


def advance(state, a_ref, b_ref, scale):
    left, right = state
    m = len(left)
    new_left, new_right = [], []
    for k in range(m):
        u, v = left[k], right[k]
        above = [
            pltpu.roll(half[m - 1], 1, 0) if k == 0 else half[k - 1] for half in state
        ]
        below = [
            pltpu.roll(half[0], 7, 0) if k == m - 1 else half[k + 1] for half in state
        ]
        su = above[0] + below[0] + (v + pltpu.roll(v, 1, 1))
        sv = above[1] + below[1] + (u + pltpu.roll(u, LANES - 1, 1))
        new_left.append(scale * su + u * (a_ref[0, k] - b_ref[0, k] * (u * u)))
        new_right.append(scale * sv + v * (a_ref[1, k] - b_ref[1, k] * (v * v)))
    return new_left, new_right


def load_rows(ref, m):
    return [[ref[h, pl.ds(k, 8, stride=m), :] for k in range(m)] for h in range(2)]


def store_rows(ref, state, first=0):
    m = len(state[0])
    for h in range(2):
        for k in range(m):
            ref[h, pl.ds(first + k, 8, stride=m), :] = state[h][k]


def load_state(ref):
    return [[ref[h, k] for k in range(ref.shape[1])] for h in range(2)]


def store_state(ref, state):
    for h in range(2):
        for k in range(len(state[h])):
            ref[h, k] = state[h][k]


def plus(state, addend):
    return [[x + y for x, y in zip(s, t)] for s, t in zip(state, addend)]


def minus(state, addend):
    return [[x - y for x, y in zip(s, t)] for s, t in zip(state, addend)]


def repeat(state, a_ref, b_ref, scale, count, unroll):
    def turn(_, carried):
        carried = [list(half) for half in carried]
        for _ in range(unroll):
            carried = advance(carried, a_ref, b_ref, scale)
        return tuple(tuple(half) for half in carried)

    state = tuple(tuple(half) for half in state)
    state = lax.fori_loop(0, count // unroll, turn, state)
    return [list(half) for half in state]


def widen(ext, values):
    for h in range(2):
        part = values[:, h * LANES : (h + 1) * LANES]
        ext[h, HALO : HALO + N] = part
        ext[h, 0:HALO] = part[N - HALO :]
        ext[h, HALO + N :] = part[:HALO]


def copy_strip(dst, ext, first, rows=ROWS):
    for h in range(2):
        for row in range(0, rows, 8):
            src = pl.ds(pl.multiple_of(first + row, 8), 8)
            dst[h, row : row + 8] = ext[h, src]


def kernel(
    init_ref,
    rate_ref,
    guess_ref,
    points_ref,
    corner_ref,
    init_in,
    rate_in,
    prior_in,
    perm,
    init_ext,
    rate_ext,
    relaxed_ext,
    strip,
    a_full,
    b_full,
    a_1,
    b_1,
    a_16,
    b_16,
    a_64,
    b_64,
    starts,
    terms,
    corner_rows,
    corner_full,
    fresh,
    ct_rows,
    ct,
    cts,
    history,
    half_history,
    half_strip,
    a_half,
    b_half,
    hop_rows,
    z_stage,
    pass_rows,
    z_in,
    z_own,
    point_rows,
    points_full,
    in_sem,
    start_send,
    start_recv,
    forward_send,
    corner_send,
    corner_recv,
    fresh_send,
    fresh_recv,
    ct_send,
    ct_recv,
    hop_send,
    hop_recv,
    pass_send,
    pass_recv,
    point_send,
    point_recv,
):
    group = lax.axis_index("tm")
    member = lax.axis_index("grp")
    groups = 32
    x, y, c = group // 8, (group // 2) % 4, group % 2
    stage = x // 2
    chip_x = x % 2
    local_group = group % STAGE
    core0 = c == 0
    mine = (x + y) % 2
    half_first = HALO - EDGE + HALF * mine

    def around(distance):
        return (member + distance) % 4

    first = jnp.logical_and(group == 0, member == 0)
    rate_copy = pltpu.make_async_copy(rate_ref, rate_in, in_sem.at[0])
    rate_copy.start()
    prior_copies = (
        pltpu.make_async_copy(init_ref, prior_in, in_sem.at[1]),
        pltpu.make_async_copy(guess_ref.at[0], prior_in, in_sem.at[1]),
    )
    pl.when(first)(prior_copies[0].start)
    pl.when(jnp.logical_not(first))(prior_copies[1].start)
    init_copy = pltpu.make_async_copy(init_ref, init_in, in_sem.at[2])
    init_copy.start()

    barrier = pltpu.get_barrier_semaphore()

    def greet(tm, grp):
        pl.semaphore_signal(barrier, inc=1, device_id=(tm, grp), device_id_type=MESH)

    for d in (1, 2, 3):
        greet(group, around(d))

    @pl.when(group > 0)
    def _():
        greet(group - 1, 3)
        greet(group - 1, member)

    @pl.when(core0)
    def _():
        for dx in range(2):
            for dy in range(4):
                px, py = stage * 2 + (chip_x + dx) % 2, (y + dy) % 4
                if (dx, dy) != (0, 0):
                    greet(at_xy(px, py, 0), member)
                greet(at_xy(px, py, 1), member)

    @pl.when(jnp.logical_and(core0, stage == 1))
    def _():
        for dy in (0, 3):
            py = (y + dy) % 4
            greet(at_xy(3 - x, py, 0), member)
            greet(at_xy(3 - x, py, 0), around(1 + 2 * ((3 - x + py) % 2)))

    @pl.when(c == 1)
    def _():
        greet(group - 1, member)

    @pl.when(stage == 0)
    def _():
        greet(at_xy(1 - x, y, 0), member)

    more = (group < groups - 1).astype(jnp.int32)
    expected = (
        3
        + more * (1 + 4 * (member == 3).astype(jnp.int32))
        + 7
        + c
        + (1 - c) * (1 + 6 * (1 - stage))
    )

    perm[...] = permutation(False)
    rate_copy.wait()
    rate = permuted(rate_in[...], perm[...])
    widen(rate_ext, rate)
    prior_copies[1].wait()
    prior = permuted(prior_in[...], perm[...])
    for h in range(2):
        relaxed_ext[h, HALO : HALO + N] = prior[:, h * LANES : (h + 1) * LANES]
    full = relaxed_ext.at[:, HALO : HALO + N]
    rates = load_rows(rate_ext.at[:, HALO : HALO + N], MF)
    for h in range(2):
        for k in range(MF):
            a_full[h, k] = (1.0 - 4.0 * KAPPA) + rates[h][k]
            b_full[h, k] = rates[h][k]
    relaxed = repeat(load_rows(full, MF), a_full, b_full, KAPPA, STEPS, 8)
    store_rows(relaxed_ext, relaxed, HALO)
    for h in range(2):
        relaxed_ext[h, 0:HALO] = relaxed_ext[h, N : N + HALO]
        relaxed_ext[h, HALO + N :] = relaxed_ext[h, HALO : 2 * HALO]

    pl.semaphore_wait(barrier, expected)

    pending = []
    slot = (member + 1) % 4
    target = group + (member == 3).astype(jnp.int32)
    have = jnp.logical_or(member < 3, group < groups - 1)
    for n, (d, part, low, high) in enumerate(
        (
            (1, 0, 64, 104),
            (3, 0, 40, 80),
            (1, 1, 104, ROWS),
            (3, 1, 0, 40),
            (1, 2, 0, 64),
            (3, 2, 80, ROWS),
            (0, 0, 0, ROWS),
        )
    ):
        q = around(d)
        copy = pltpu.make_async_remote_copy(
            src_ref=relaxed_ext.at[
                :, pl.ds(pl.multiple_of(q * CORE + low, 8), high - low)
            ],
            dst_ref=starts.at[slot, :, low:high],
            send_sem=start_send.at[n],
            recv_sem=start_recv.at[slot, part],
            device_id=(target, q),
            device_id_type=MESH,
        )
        when = have if d else jnp.logical_and(have, member == 3)
        pl.when(when)(copy.start)
        pending.append((when, copy))

    own_first = pl.multiple_of(member * CORE, 8)

    @pl.when(member < 3)
    def _():
        copy_strip(starts.at[slot], relaxed_ext, own_first)

    init_copy.wait()
    widen(init_ext, permuted(init_in[...], perm[...]))

    @pl.when(group == 0)
    def _():
        copy_strip(starts.at[0], init_ext, own_first)
        copy_strip(fresh, init_ext, own_first)

    copy_strip(strip, rate_ext, own_first)
    rates = load_rows(strip, M)
    for h in range(2):
        for k in range(M):
            r = rates[h][k]
            for factor, a_ref, b_ref in (
                (1.0, a_1, b_1),
                (16.0, a_16, b_16),
                (64.0, a_64, b_64),
            ):
                a_ref[h, k] = (1.0 - 4.0 * KAPPA * factor) + factor * r
                b_ref[h, k] = factor * r
    copy_strip(strip, init_ext, own_first)
    perm[...] = permutation(True)

    @pl.when(jnp.logical_and(core0, stage == 0))
    def _():
        first_row = own_first + half_first
        copy_strip(half_strip, rate_ext, first_row, HALF_ROWS)
        rates = load_rows(half_strip, MH)
        for h in range(2):
            for k in range(MH):
                r = 64.0 * rates[h][k]
                a_half[h, k] = (1.0 - 4.0 * KAPPA * 64.0) + r
                b_half[h, k] = r
        copy_strip(half_strip, init_ext, first_row, HALF_ROWS)

    def arrived(s, low, high, part):
        pltpu.make_async_remote_copy(
            src_ref=starts.at[s, :, low:high],
            dst_ref=starts.at[s, :, low:high],
            send_sem=start_send.at[0],
            recv_sem=start_recv.at[s, part],
            device_id=(group, around(1)),
            device_id_type=MESH,
        ).wait_recv()

    def make_terms(slots, unroll=8):
        for s in slots:
            start = load_rows(starts.at[s], M)
            store_state(terms.at[s], advance(start, a_16, b_16, 16.0 * KAPPA))

        def turn(_, carried):
            for _ in range(unroll):
                carried = [advance(state, a_1, b_1, KAPPA) for state in carried]
            return tuple(tuple(tuple(half) for half in state) for state in carried)

        carried = tuple(
            tuple(tuple(half) for half in load_rows(starts.at[s], M)) for s in slots
        )
        fine = lax.fori_loop(0, STEPS // unroll, turn, carried)
        for s, state in zip(slots, fine):
            store_state(terms.at[s], minus(state, load_state(terms.at[s])))

    below, above, far = (slot + 3) % 4, (slot + 1) % 4, (slot + 2) % 4

    def there(s):
        return jnp.logical_or(s != 0, group > 0)

    @pl.when(member < 3)
    def _():
        make_terms([slot])

    pieces = (
        (below, 0, 64, 104, 64, 40, 0, 0, 1),
        (above, 0, 40, 80, 40, 40, 104, 1, 3),
        (below, 1, 104, ROWS, 104, 32, 40, 2, 1),
        (above, 1, 0, 40, 8, 32, 72, 3, 3),
    )
    for s, part, low, high, src, count, dst, to, d in pieces:
        copy = pltpu.make_async_remote_copy(
            src_ref=starts.at[s, :, src : src + count],
            dst_ref=starts.at[s, :, dst : dst + count],
            send_sem=forward_send.at[to],
            recv_sem=start_recv.at[s, to],
            device_id=(group, around(d)),
            device_id_type=MESH,
        )

        @pl.when(there(s))
        def _(s=s, part=part, low=low, high=high, copy=copy):
            arrived(s, low, high, part)
            copy.start()

        pending.append((there(s), copy))

    @pl.when(member == 3)
    def _():
        @pl.when(group > 0)
        def _():
            arrived(slot, 0, ROWS, 0)

        make_terms([slot])

    @pl.when(there(below))
    def _():
        arrived(below, 0, 64, 2)

    @pl.when(there(above))
    def _():
        arrived(above, 80, ROWS, 2)

    make_terms([below, above])

    @pl.when(there(far))
    def _():
        for first_row, count, n in ((0, 40, 0), (104, 40, 1), (40, 32, 2), (72, 32, 3)):
            arrived(far, first_row, first_row + count, n)

    make_terms([far], 16)

    def big_step(state, index):
        stepped = advance(state, a_16, b_16, 16.0 * KAPPA)
        return plus(stepped, load_state(terms.at[index]))

    corner = load_rows(starts.at[0], M)
    for index in range(4):
        corner = big_step(corner, index)
    store_rows(corner_rows, corner)
    sent = slice(HALO - 24, HALO + CORE + 24)
    fresh_copies = []
    for h in range(1):
        copy = pltpu.make_async_remote_copy(
            src_ref=corner_rows.at[:, sent],
            dst_ref=fresh.at[:, sent],
            send_sem=fresh_send.at[h],
            recv_sem=fresh_recv.at[h],
            device_id=(lax.rem(group + 1, groups), member),
            device_id_type=MESH,
        )
        fresh_copies.append(copy)
        pl.when(group < groups - 1)(copy.start)
        pending.append((group < groups - 1, copy))
    core_rows = slice(HALO, HALO + CORE)
    own_rows = pl.ds(own_first, CORE)
    for d in (1, 3, 2):
        copy = pltpu.make_async_remote_copy(
            src_ref=corner_rows.at[:, core_rows],
            dst_ref=corner_full.at[:, own_rows],
            send_sem=corner_send.at[d - 1],
            recv_sem=corner_recv.at[member],
            device_id=(group, around(d)),
            device_id_type=MESH,
        )
        copy.start()
        pending.append((None, copy))
    for h in range(2):
        corner_full[h, own_rows] = corner_rows[h, core_rows]

    for copy in fresh_copies:
        pl.when(group > 0)(copy.wait_recv)
    state = load_rows(fresh, M)
    for index in range(4):
        state = big_step(state, index)
    state = minus(state, advance(load_rows(fresh, M), a_64, b_64, 64.0 * KAPPA))
    store_state(ct, state)
    store_rows(ct_rows, state)
    def ct_copies(halo, of_stage):
        copies = []
        for dx in (1, 0):
            for dy in (2, 1, 3, 0):
                px, py = of_stage * 2 + (chip_x + dx) % 2, (y + dy) % 4
                if of_stage:
                    src = dst = slice(HALO - halo, HALO + CORE + halo)
                else:
                    its_first = HALO - halo + HALF * ((px + py) % 2)
                    src = pl.ds(pl.multiple_of(its_first, 8), HALF + 2 * halo)
                    dst = slice(EDGE - halo, EDGE + HALF + halo)
                copies.append(
                    pltpu.make_async_remote_copy(
                        src_ref=ct_rows.at[:, src],
                        dst_ref=cts.at[local_group, :, dst],
                        send_sem=ct_send.at[dx * 4 + dy],
                        recv_sem=ct_recv.at[local_group],
                        device_id=(at_xy(px, py, 0), member),
                        device_id_type=MESH,
                    )
                )
        return copies

    widths = (
        (24, local_group == 0),
        (16, jnp.logical_and(local_group > 0, local_group <= 8)),
        (8, jnp.logical_and(local_group > 8, group < groups - 1)),
    )
    for halo, when in widths:
        for of_stage in range(2):

            @pl.when(jnp.logical_and(when, stage == of_stage))
            def _(halo=halo, of_stage=of_stage):
                copies = ct_copies(halo, of_stage)
                for copy in copies[:-1]:
                    copy.start()
                pl.when(c == 1)(copies[-1].start)

    for d in (1, 3, 2):
        q = around(d)
        pltpu.make_async_remote_copy(
            src_ref=corner_rows.at[:, core_rows],
            dst_ref=corner_full.at[:, pl.ds(pl.multiple_of(q * CORE, 8), CORE)],
            send_sem=corner_send.at[0],
            recv_sem=corner_recv.at[q],
            device_id=(group, q),
            device_id_type=MESH,
        ).wait_recv()
    both = jnp.concatenate([corner_full[0], corner_full[1]], axis=1)
    corner_ref[...] = permuted(both, perm[...])

    def remote(src, dst, send, recv, tm, grp=member):
        return pltpu.make_async_remote_copy(
            src_ref=src,
            dst_ref=dst,
            send_sem=send,
            recv_sem=recv,
            device_id=(tm, grp),
            device_id_type=MESH,
        )

    def rows_at(first, count):
        return pl.ds(pl.multiple_of(first, 8), count)

    hop = []
    for dy in (1, 0):
        tm = at_xy(3 - x, (y + dy) % 4, 0)
        hop.append(
            remote(
                hop_rows.at[:, rows_at(EDGE + 8 * mine, EDGE)],
                z_stage.at[:, rows_at(HALO + CORE - (CORE + EDGE) * mine, EDGE)],
                hop_send.at[2 * dy],
                hop_recv.at[2 + mine],
                tm,
                around(3 - 2 * mine),
            )
        )
        hop.append(
            remote(
                hop_rows.at[:, EDGE : EDGE + HALF],
                z_stage.at[:, rows_at(HALO + HALF * mine, HALF)],
                hop_send.at[2 * dy + 1],
                hop_recv.at[mine],
                tm,
            )
        )
    hop_arrivals = []
    for n, (first, count) in enumerate(
        (
            (HALO, HALF),
            (HALO + HALF, HALF),
            (HALO + CORE, EDGE),
            (HALO - EDGE, EDGE),
        )
    ):
        there_rows = z_stage.at[:, first : first + count]
        hop_arrivals.append(
            remote(there_rows, there_rows, hop_send.at[0], hop_recv.at[n], group)
        )

    handed = slice(HALO - 8, HALO + CORE + 8)
    sibling = at_xy(x, y, 1)
    pass_copy = remote(
        pass_rows.at[0, :, handed],
        z_in.at[:, handed],
        pass_send.at[0],
        pass_recv.at[0],
        sibling,
    )
    part = HALF + 8
    half_src, half_dst = 16 + 8 * mine, HALO - 8 + part * mine
    given = []
    for n, tm in enumerate((sibling, at_xy(1 - x, y, 0), at_xy(1 - x, y, 1))):
        given.append(
            remote(
                pass_rows.at[n, :, rows_at(half_src, part)],
                z_in.at[:, rows_at(half_dst, part)],
                pass_send.at[n],
                pass_recv.at[mine],
                tm,
            )
        )

    def half_arrived(which):
        there_rows = z_in.at[:, rows_at(HALO - 8 + part * which, part)]
        remote(
            there_rows, there_rows, pass_send.at[0], pass_recv.at[which], group
        ).wait_recv()

    def chain(begin, a_ref, b_ref, core, states, edge, steps):
        last = begin
        m = len(begin[0])
        for t in range(steps):
            if t % 4 == 0:
                for n in range(t, min(t + 4, steps)):
                    halo = 24 if n == 0 else 16 if n <= 8 else 8
                    rows = cts.at[n, :, edge - halo : edge + core + halo]

                    @pl.when(n != local_group)
                    def _(n=n, rows=rows):
                        remote(
                            rows, rows, ct_send.at[0], ct_recv.at[n], sibling
                        ).wait_recv()

            last = advance(last, a_ref, b_ref, 64.0 * KAPPA)
            last = plus(last, load_rows(cts.at[t, :, 0 : 8 * m], m))
            store_state(states.at[t + 1], last)
        return last

    @pl.when(jnp.logical_and(core0, stage == 0))
    def _():
        copy_strip(cts.at[local_group], ct_rows.at[:, :], half_first, HALF_ROWS)
        begin = load_rows(half_strip, MH)
        store_state(half_history.at[0], begin)
        last = chain(begin, a_half, b_half, HALF, half_history, EDGE, STAGE)
        store_rows(hop_rows, last)
        for copy in hop:
            copy.start()
        other = (local_group + STAGE // 2) % STAGE
        for n, t in enumerate((local_group + 1, other, other + 1)):
            store_rows(pass_rows.at[n], load_state(half_history.at[t]))
            given[n].start()
        store_rows(half_strip, load_state(half_history.at[local_group]))
        for h in range(2):
            z_in[h, rows_at(half_dst, part)] = half_strip[h, rows_at(half_src, part)]

    @pl.when(jnp.logical_and(core0, stage == 1))
    def _():
        store_rows(cts.at[local_group], load_state(ct))
        for copy in hop_arrivals:
            copy.wait_recv()
        begin = load_rows(z_stage, M)
        store_state(history.at[0], begin)
        chain(begin, a_64, b_64, CORE, history, HALO, STAGE - 1)
        store_rows(pass_rows.at[0], load_state(history.at[local_group + 1]))
        pass_copy.start()
        store_state(z_own, load_state(history.at[local_group]))

    @pl.when(stage == 0)
    def _():
        half_arrived(1 - mine)
        pl.when(c == 1)(lambda: half_arrived(mine))
        store_state(z_own, load_rows(z_in, M))

    @pl.when(jnp.logical_and(c == 1, stage == 1))
    def _():
        pass_copy.wait_recv()
        store_state(z_own, load_rows(z_in, M))

    final = load_state(z_own)
    final = plus(advance(final, a_64, b_64, 64.0 * KAPPA), load_state(ct))
    state = load_state(z_own)
    for index in (3, 0, 1, 2):
        if index < 3:
            state = big_step(state, index)
        store_rows(point_rows.at[index], state if index < 3 else final)

        copy = pltpu.make_async_remote_copy(
            src_ref=point_rows.at[index, :, core_rows],
            dst_ref=points_full.at[:, own_rows],
            send_sem=point_send.at[index],
            recv_sem=point_recv.at[member],
            device_id=(group, index),
            device_id_type=MESH,
        )
        when = member != index
        pl.when(when)(copy.start)
        pending.append((when, copy))
    for h in range(2):
        points_full[h, own_rows] = point_rows[member, h, core_rows]
    for d in (0, 1, 3, 2):
        q = around(d)
        rows = pl.ds(pl.multiple_of(q * CORE, 8), CORE)
        if d:
            pltpu.make_async_remote_copy(
                src_ref=point_rows.at[0, :, core_rows],
                dst_ref=points_full.at[:, rows],
                send_sem=point_send.at[0],
                recv_sem=point_recv.at[q],
                device_id=(group, q),
                device_id_type=MESH,
            ).wait_recv()
        both = jnp.concatenate([points_full[0, rows], points_full[1, rows]], axis=1)
        points_ref[rows] = permuted(both, perm[...])

    for when, copy in pending:
        if when is None:
            copy.wait_send()
        else:
            pl.when(when)(copy.wait_send)

    for halo, when in widths:
        for of_stage in range(2):

            @pl.when(jnp.logical_and(when, stage == of_stage))
            def _(halo=halo, of_stage=of_stage):
                copies = ct_copies(halo, of_stage)
                for copy in copies[:-1]:
                    copy.wait_send()
                pl.when(c == 1)(copies[-1].wait_send)

    @pl.when(jnp.logical_and(core0, stage == 0))
    def _():
        for copy in hop + given:
            copy.wait_send()

    @pl.when(jnp.logical_and(core0, stage == 1))
    def _():
        pass_copy.wait_send()


def write_out(points, corner, points_out, corner_out, sems):
    copies = (
        pltpu.make_async_copy(points, points_out.at[0], sems.at[0]),
        pltpu.make_async_copy(corner, corner_out.at[0], sems.at[1]),
    )
    for copy in copies:
        copy.start()
    for copy in copies:
        copy.wait()


def local(init_field, reaction, guesses):
    vmem = pl.BlockSpec(memory_space=pltpu.VMEM)
    strip_state = pltpu.VMEM((2, M, 8, LANES), F32)
    full_state = pltpu.VMEM((2, MF, 8, LANES), F32)
    strip_rows = pltpu.VMEM((2, ROWS, LANES), F32)
    ext_rows = pltpu.VMEM((2, N + 2 * HALO, LANES), F32)
    full_rows = pltpu.VMEM((2, N, LANES), F32)
    dma = pltpu.SemaphoreType.DMA

    def many(count, *shape):
        return pltpu.VMEM((count, *shape), F32)

    scratch = [
        *[pltpu.VMEM((N, N), F32)] * 3,
        pltpu.VMEM((N, N), jnp.bfloat16),
        ext_rows,
        ext_rows,
        ext_rows,
        strip_rows,
        full_state,
        full_state,
        *[strip_state] * 6,
        many(4, 2, ROWS, LANES),
        many(4, 2, M, 8, LANES),
        strip_rows,
        full_rows,
        strip_rows,
        strip_rows,
        strip_state,
        many(STAGE, 2, ROWS, LANES),
        many(STAGE + 1, 2, M, 8, LANES),
        many(STAGE + 1, 2, MH, 8, LANES),
        pltpu.VMEM((2, HALF_ROWS, LANES), F32),
        *[pltpu.VMEM((2, MH, 8, LANES), F32)] * 2,
        pltpu.VMEM((2, HALF_ROWS, LANES), F32),
        strip_rows,
        many(3, 2, ROWS, LANES),
        strip_rows,
        strip_state,
        many(4, 2, ROWS, LANES),
        full_rows,
        dma((3,)),
        dma((8,)),
        dma((4, 4)),
        dma((4,)),
        dma((3,)),
        dma((4,)),
        dma((2,)),
        dma((2,)),
        dma((8,)),
        dma((STAGE,)),
        dma((4,)),
        dma((4,)),
        dma((3,)),
        dma((2,)),
        dma((4,)),
        dma((4,)),
    ]
    hbm = pl.BlockSpec(memory_space=pltpu.HBM)
    points, corner = pl.pallas_call(
        kernel,
        out_shape=(
            jax.ShapeDtypeStruct((N, N), F32),
            jax.ShapeDtypeStruct((N, N), F32),
        ),
        in_specs=[hbm] * 3,
        out_specs=(vmem, vmem),
        scratch_shapes=scratch,
        compiler_params=pltpu.CompilerParams(
            collective_id=0, has_side_effects=True, vmem_limit_bytes=213 * 2**18
        ),
    )(init_field, reaction, guesses)
    block = jax.ShapeDtypeStruct((1, N, N), F32)
    return pl.pallas_call(
        write_out,
        out_shape=(block, block),
        in_specs=[vmem] * 2,
        out_specs=(hbm, hbm),
        scratch_shapes=[dma((2,))],
        compiler_params=pltpu.CompilerParams(vmem_limit_bytes=8 * 2**20),
    )(points, corner)


def solution(mesh):
    return jax.shard_map(
        local,
        mesh=mesh,
        in_specs=(P(), P(), P(("tm", "grp"), None, None)),
        out_specs=(P(("tm", "grp"), None, None), P("tm", None, None)),
        check_vma=False,
    )
```

```python
import functools

import jax
import jax.numpy as jnp
from jax import lax
from jax.experimental import pallas as pl
from jax.experimental.pallas import tpu as pltpu
from jax.sharding import PartitionSpec as P

STEPS = 16
KAPPA = 0.0035
MESH = pl.DeviceIdType.MESH

N = 256
LANES = 128
HALO = 40
CORE = 64
ROWS = CORE + 2 * HALO
M = ROWS // 8
MF = N // 8
STAGE = 16
HALF = CORE // 2
EDGE = 24
HALF_ROWS = HALF + 2 * EDGE
MH = HALF_ROWS // 8
F32 = jnp.float32


def at_xy(x, y, c):
    return (x * 4 + y) * 2 + c


def permutation(transposed):
    big = lax.broadcasted_iota(jnp.int32, (N, N), 1 if transposed else 0)
    new = lax.broadcasted_iota(jnp.int32, (N, N), 0 if transposed else 1)
    wanted = 2 * (new % LANES) + new // LANES
    return (big == wanted).astype(F32).astype(jnp.bfloat16)


def permuted(values, matrix):
    high = values.astype(jnp.bfloat16)
    rest = values - high.astype(F32)
    middle = rest.astype(jnp.bfloat16)
    low = (rest - middle.astype(F32)).astype(jnp.bfloat16)
    parts = jnp.concatenate([high, middle, low], axis=0)
    moved = jnp.dot(parts, matrix, preferred_element_type=F32)
    rows = values.shape[0]
    return (moved[:rows] + moved[rows : 2 * rows]) + moved[2 * rows :]


def advance(state, a_ref, b_ref, scale):
    left, right = state
    m = len(left)
    new_left, new_right = [], []
    for k in range(m):
        u, v = left[k], right[k]
        above = [
            pltpu.roll(half[m - 1], 1, 0) if k == 0 else half[k - 1] for half in state
        ]
        below = [
            pltpu.roll(half[0], 7, 0) if k == m - 1 else half[k + 1] for half in state
        ]
        su = above[0] + below[0] + (v + pltpu.roll(v, 1, 1))
        sv = above[1] + below[1] + (u + pltpu.roll(u, LANES - 1, 1))
        new_left.append(scale * su + u * (a_ref[0, k] - b_ref[0, k] * (u * u)))
        new_right.append(scale * sv + v * (a_ref[1, k] - b_ref[1, k] * (v * v)))
    return new_left, new_right


def load_rows(ref, m):
    return [[ref[h, pl.ds(k, 8, stride=m), :] for k in range(m)] for h in range(2)]


def store_rows(ref, state, first=0):
    m = len(state[0])
    for h in range(2):
        for k in range(m):
            ref[h, pl.ds(first + k, 8, stride=m), :] = state[h][k]


def load_state(ref):
    return [[ref[h, k] for k in range(ref.shape[1])] for h in range(2)]


def store_state(ref, state):
    for h in range(2):
        for k in range(len(state[h])):
            ref[h, k] = state[h][k]


def plus(state, addend):
    return [[x + y for x, y in zip(s, t)] for s, t in zip(state, addend)]


def minus(state, addend):
    return [[x - y for x, y in zip(s, t)] for s, t in zip(state, addend)]


def repeat(state, a_ref, b_ref, scale, count, unroll):
    def turn(_, carried):
        carried = [list(half) for half in carried]
        for _ in range(unroll):
            carried = advance(carried, a_ref, b_ref, scale)
        return tuple(tuple(half) for half in carried)

    state = tuple(tuple(half) for half in state)
    state = lax.fori_loop(0, count // unroll, turn, state)
    return [list(half) for half in state]


def widen(ext, values):
    for h in range(2):
        part = values[:, h * LANES : (h + 1) * LANES]
        ext[h, HALO : HALO + N] = part
        ext[h, 0:HALO] = part[N - HALO :]
        ext[h, HALO + N :] = part[:HALO]


def copy_strip(dst, ext, first, rows=ROWS):
    for h in range(2):
        for row in range(0, rows, 8):
            src = pl.ds(pl.multiple_of(first + row, 8), 8)
            dst[h, row : row + 8] = ext[h, src]


def kernel(
    init_ref,
    rate_ref,
    guess_ref,
    points_ref,
    corner_ref,
    init_in,
    rate_in,
    prior_in,
    perm,
    init_ext,
    rate_ext,
    relaxed_ext,
    strip,
    a_full,
    b_full,
    a_1,
    b_1,
    a_16,
    b_16,
    a_64,
    b_64,
    starts,
    terms,
    corner_rows,
    corner_full,
    fresh,
    ct_rows,
    ct,
    cts,
    history,
    half_history,
    half_strip,
    a_half,
    b_half,
    hop_rows,
    z_stage,
    pass_rows,
    z_in,
    z_own,
    point_rows,
    points_full,
    in_sem,
    start_send,
    start_recv,
    forward_send,
    corner_send,
    corner_recv,
    fresh_send,
    fresh_recv,
    ct_send,
    ct_recv,
    hop_send,
    hop_recv,
    pass_send,
    pass_recv,
    point_send,
    point_recv,
):
    group = lax.axis_index("tm")
    member = lax.axis_index("grp")
    groups = 32
    x, y, c = group // 8, (group // 2) % 4, group % 2
    stage = x // 2
    chip_x = x % 2
    local_group = group % STAGE
    core0 = c == 0
    mine = (x + y) % 2
    half_first = HALO - EDGE + HALF * mine

    def around(distance):
        return (member + distance) % 4

    first = jnp.logical_and(group == 0, member == 0)
    rate_copy = pltpu.make_async_copy(rate_ref, rate_in, in_sem.at[0])
    rate_copy.start()
    prior_copies = (
        pltpu.make_async_copy(init_ref, prior_in, in_sem.at[1]),
        pltpu.make_async_copy(guess_ref.at[0], prior_in, in_sem.at[1]),
    )
    pl.when(first)(prior_copies[0].start)
    pl.when(jnp.logical_not(first))(prior_copies[1].start)
    init_copy = pltpu.make_async_copy(init_ref, init_in, in_sem.at[2])
    init_copy.start()

    barrier = pltpu.get_barrier_semaphore()

    def greet(tm, grp):
        pl.semaphore_signal(barrier, inc=1, device_id=(tm, grp), device_id_type=MESH)

    for d in (1, 2, 3):
        greet(group, around(d))

    @pl.when(group > 0)
    def _():
        greet(group - 1, 3)
        greet(group - 1, member)

    @pl.when(core0)
    def _():
        for dx in range(2):
            for dy in range(4):
                px, py = stage * 2 + (chip_x + dx) % 2, (y + dy) % 4
                if (dx, dy) != (0, 0):
                    greet(at_xy(px, py, 0), member)
                greet(at_xy(px, py, 1), member)

    @pl.when(jnp.logical_and(core0, stage == 1))
    def _():
        for dy in (0, 3):
            py = (y + dy) % 4
            greet(at_xy(3 - x, py, 0), member)
            greet(at_xy(3 - x, py, 0), around(1 + 2 * ((3 - x + py) % 2)))

    @pl.when(c == 1)
    def _():
        greet(group - 1, member)

    @pl.when(stage == 0)
    def _():
        greet(at_xy(1 - x, y, 0), member)

    more = (group < groups - 1).astype(jnp.int32)
    expected = (
        3
        + more * (1 + 4 * (member == 3).astype(jnp.int32))
        + 7
        + c
        + (1 - c) * (1 + 6 * (1 - stage))
    )

    perm[...] = permutation(False)
    rate_copy.wait()
    rate = permuted(rate_in[...], perm[...])
    widen(rate_ext, rate)
    prior_copies[1].wait()
    prior = permuted(prior_in[...], perm[...])
    for h in range(2):
        relaxed_ext[h, HALO : HALO + N] = prior[:, h * LANES : (h + 1) * LANES]
    full = relaxed_ext.at[:, HALO : HALO + N]
    rates = load_rows(rate_ext.at[:, HALO : HALO + N], MF)
    for h in range(2):
        for k in range(MF):
            a_full[h, k] = (1.0 - 4.0 * KAPPA) + rates[h][k]
            b_full[h, k] = rates[h][k]
    relaxed = repeat(load_rows(full, MF), a_full, b_full, KAPPA, STEPS, 8)
    store_rows(relaxed_ext, relaxed, HALO)
    for h in range(2):
        relaxed_ext[h, 0:HALO] = relaxed_ext[h, N : N + HALO]
        relaxed_ext[h, HALO + N :] = relaxed_ext[h, HALO : 2 * HALO]

    pl.semaphore_wait(barrier, expected)

    pending = []
    slot = (member + 1) % 4
    target = group + (member == 3).astype(jnp.int32)
    have = jnp.logical_or(member < 3, group < groups - 1)
    for n, (d, part, low, high) in enumerate(
        (
            (1, 0, 64, 104),
            (3, 0, 40, 80),
            (1, 1, 104, ROWS),
            (3, 1, 0, 40),
            (1, 2, 0, 64),
            (3, 2, 80, ROWS),
            (0, 0, 0, ROWS),
        )
    ):
        q = around(d)
        copy = pltpu.make_async_remote_copy(
            src_ref=relaxed_ext.at[
                :, pl.ds(pl.multiple_of(q * CORE + low, 8), high - low)
            ],
            dst_ref=starts.at[slot, :, low:high],
            send_sem=start_send.at[n],
            recv_sem=start_recv.at[slot, part],
            device_id=(target, q),
            device_id_type=MESH,
        )
        when = have if d else jnp.logical_and(have, member == 3)
        pl.when(when)(copy.start)
        pending.append((when, copy))

    own_first = pl.multiple_of(member * CORE, 8)

    @pl.when(member < 3)
    def _():
        copy_strip(starts.at[slot], relaxed_ext, own_first)

    init_copy.wait()
    widen(init_ext, permuted(init_in[...], perm[...]))

    @pl.when(group == 0)
    def _():
        copy_strip(starts.at[0], init_ext, own_first)
        copy_strip(fresh, init_ext, own_first)

    copy_strip(strip, rate_ext, own_first)
    rates = load_rows(strip, M)
    for h in range(2):
        for k in range(M):
            r = rates[h][k]
            for factor, a_ref, b_ref in (
                (1.0, a_1, b_1),
                (16.0, a_16, b_16),
                (64.0, a_64, b_64),
            ):
                a_ref[h, k] = (1.0 - 4.0 * KAPPA * factor) + factor * r
                b_ref[h, k] = factor * r
    copy_strip(strip, init_ext, own_first)
    perm[...] = permutation(True)

    @pl.when(jnp.logical_and(core0, stage == 0))
    def _():
        first_row = own_first + half_first
        copy_strip(half_strip, rate_ext, first_row, HALF_ROWS)
        rates = load_rows(half_strip, MH)
        for h in range(2):
            for k in range(MH):
                r = 64.0 * rates[h][k]
                a_half[h, k] = (1.0 - 4.0 * KAPPA * 64.0) + r
                b_half[h, k] = r
        copy_strip(half_strip, init_ext, first_row, HALF_ROWS)

    def arrived(s, low, high, part):
        pltpu.make_async_remote_copy(
            src_ref=starts.at[s, :, low:high],
            dst_ref=starts.at[s, :, low:high],
            send_sem=start_send.at[0],
            recv_sem=start_recv.at[s, part],
            device_id=(group, around(1)),
            device_id_type=MESH,
        ).wait_recv()

    def make_terms(slots, unroll=8):
        for s in slots:
            start = load_rows(starts.at[s], M)
            store_state(terms.at[s], advance(start, a_16, b_16, 16.0 * KAPPA))

        def turn(_, carried):
            for _ in range(unroll):
                carried = [advance(state, a_1, b_1, KAPPA) for state in carried]
            return tuple(tuple(tuple(half) for half in state) for state in carried)

        carried = tuple(
            tuple(tuple(half) for half in load_rows(starts.at[s], M)) for s in slots
        )
        fine = lax.fori_loop(0, STEPS // unroll, turn, carried)
        for s, state in zip(slots, fine):
            store_state(terms.at[s], minus(state, load_state(terms.at[s])))

    below, above, far = (slot + 3) % 4, (slot + 1) % 4, (slot + 2) % 4

    def there(s):
        return jnp.logical_or(s != 0, group > 0)

    @pl.when(member < 3)
    def _():
        make_terms([slot])

    pieces = (
        (below, 0, 64, 104, 64, 40, 0, 0, 1),
        (above, 0, 40, 80, 40, 40, 104, 1, 3),
        (below, 1, 104, ROWS, 104, 32, 40, 2, 1),
        (above, 1, 0, 40, 8, 32, 72, 3, 3),
    )
    for s, part, low, high, src, count, dst, to, d in pieces:
        copy = pltpu.make_async_remote_copy(
            src_ref=starts.at[s, :, src : src + count],
            dst_ref=starts.at[s, :, dst : dst + count],
            send_sem=forward_send.at[to],
            recv_sem=start_recv.at[s, to],
            device_id=(group, around(d)),
            device_id_type=MESH,
        )

        @pl.when(there(s))
        def _(s=s, part=part, low=low, high=high, copy=copy):
            arrived(s, low, high, part)
            copy.start()

        pending.append((there(s), copy))

    @pl.when(member == 3)
    def _():
        @pl.when(group > 0)
        def _():
            arrived(slot, 0, ROWS, 0)

        make_terms([slot])

    @pl.when(there(below))
    def _():
        arrived(below, 0, 64, 2)

    @pl.when(there(above))
    def _():
        arrived(above, 80, ROWS, 2)

    make_terms([below, above])

    @pl.when(there(far))
    def _():
        for first_row, count, n in ((0, 40, 0), (104, 40, 1), (40, 32, 2), (72, 32, 3)):
            arrived(far, first_row, first_row + count, n)

    make_terms([far], 16)

    def big_step(state, index):
        stepped = advance(state, a_16, b_16, 16.0 * KAPPA)
        return plus(stepped, load_state(terms.at[index]))

    corner = load_rows(starts.at[0], M)
    for index in range(4):
        corner = big_step(corner, index)
    store_rows(corner_rows, corner)
    sent = slice(HALO - 24, HALO + CORE + 24)
    fresh_copies = []
    for h in range(1):
        copy = pltpu.make_async_remote_copy(
            src_ref=corner_rows.at[:, sent],
            dst_ref=fresh.at[:, sent],
            send_sem=fresh_send.at[h],
            recv_sem=fresh_recv.at[h],
            device_id=(lax.rem(group + 1, groups), member),
            device_id_type=MESH,
        )
        fresh_copies.append(copy)
        pl.when(group < groups - 1)(copy.start)
        pending.append((group < groups - 1, copy))
    core_rows = slice(HALO, HALO + CORE)
    own_rows = pl.ds(own_first, CORE)
    for d in (1, 3, 2):
        copy = pltpu.make_async_remote_copy(
            src_ref=corner_rows.at[:, core_rows],
            dst_ref=corner_full.at[:, own_rows],
            send_sem=corner_send.at[d - 1],
            recv_sem=corner_recv.at[member],
            device_id=(group, around(d)),
            device_id_type=MESH,
        )
        copy.start()
        pending.append((None, copy))
    for h in range(2):
        corner_full[h, own_rows] = corner_rows[h, core_rows]

    for copy in fresh_copies:
        pl.when(group > 0)(copy.wait_recv)
    state = load_rows(fresh, M)
    for index in range(4):
        state = big_step(state, index)
    state = minus(state, advance(load_rows(fresh, M), a_64, b_64, 64.0 * KAPPA))
    store_state(ct, state)
    store_rows(ct_rows, state)
    def ct_copies(halo, of_stage):
        copies = []
        for dx in (1, 0):
            for dy in (2, 1, 3, 0):
                px, py = of_stage * 2 + (chip_x + dx) % 2, (y + dy) % 4
                if of_stage:
                    src = dst = slice(HALO - halo, HALO + CORE + halo)
                else:
                    its_first = HALO - halo + HALF * ((px + py) % 2)
                    src = pl.ds(pl.multiple_of(its_first, 8), HALF + 2 * halo)
                    dst = slice(EDGE - halo, EDGE + HALF + halo)
                copies.append(
                    pltpu.make_async_remote_copy(
                        src_ref=ct_rows.at[:, src],
                        dst_ref=cts.at[local_group, :, dst],
                        send_sem=ct_send.at[dx * 4 + dy],
                        recv_sem=ct_recv.at[local_group],
                        device_id=(at_xy(px, py, 0), member),
                        device_id_type=MESH,
                    )
                )
        return copies

    widths = (
        (24, local_group == 0),
        (16, jnp.logical_and(local_group > 0, local_group <= 8)),
        (8, jnp.logical_and(local_group > 8, group < groups - 1)),
    )
    for halo, when in widths:
        for of_stage in range(2):

            @pl.when(jnp.logical_and(when, stage == of_stage))
            def _(halo=halo, of_stage=of_stage):
                copies = ct_copies(halo, of_stage)
                for copy in copies[:-1]:
                    copy.start()
                pl.when(c == 1)(copies[-1].start)

    for d in (1, 3, 2):
        q = around(d)
        pltpu.make_async_remote_copy(
            src_ref=corner_rows.at[:, core_rows],
            dst_ref=corner_full.at[:, pl.ds(pl.multiple_of(q * CORE, 8), CORE)],
            send_sem=corner_send.at[0],
            recv_sem=corner_recv.at[q],
            device_id=(group, q),
            device_id_type=MESH,
        ).wait_recv()
    both = jnp.concatenate([corner_full[0], corner_full[1]], axis=1)
    corner_ref[...] = permuted(both, perm[...])

    def remote(src, dst, send, recv, tm, grp=member):
        return pltpu.make_async_remote_copy(
            src_ref=src,
            dst_ref=dst,
            send_sem=send,
            recv_sem=recv,
            device_id=(tm, grp),
            device_id_type=MESH,
        )

    def rows_at(first, count):
        return pl.ds(pl.multiple_of(first, 8), count)

    hop = []
    for dy in (1, 0):
        tm = at_xy(3 - x, (y + dy) % 4, 0)
        hop.append(
            remote(
                hop_rows.at[:, rows_at(EDGE + 8 * mine, EDGE)],
                z_stage.at[:, rows_at(HALO + CORE - (CORE + EDGE) * mine, EDGE)],
                hop_send.at[2 * dy],
                hop_recv.at[2 + mine],
                tm,
                around(3 - 2 * mine),
            )
        )
        hop.append(
            remote(
                hop_rows.at[:, EDGE : EDGE + HALF],
                z_stage.at[:, rows_at(HALO + HALF * mine, HALF)],
                hop_send.at[2 * dy + 1],
                hop_recv.at[mine],
                tm,
            )
        )
    hop_arrivals = []
    for n, (first, count) in enumerate(
        (
            (HALO, HALF),
            (HALO + HALF, HALF),
            (HALO + CORE, EDGE),
            (HALO - EDGE, EDGE),
        )
    ):
        there_rows = z_stage.at[:, first : first + count]
        hop_arrivals.append(
            remote(there_rows, there_rows, hop_send.at[0], hop_recv.at[n], group)
        )

    handed = slice(HALO - 8, HALO + CORE + 8)
    sibling = at_xy(x, y, 1)
    pass_copy = remote(
        pass_rows.at[0, :, handed],
        z_in.at[:, handed],
        pass_send.at[0],
        pass_recv.at[0],
        sibling,
    )
    part = HALF + 8
    half_src, half_dst = 16 + 8 * mine, HALO - 8 + part * mine
    given = []
    for n, tm in enumerate((sibling, at_xy(1 - x, y, 0), at_xy(1 - x, y, 1))):
        given.append(
            remote(
                pass_rows.at[n, :, rows_at(half_src, part)],
                z_in.at[:, rows_at(half_dst, part)],
                pass_send.at[n],
                pass_recv.at[mine],
                tm,
            )
        )

    def half_arrived(which):
        there_rows = z_in.at[:, rows_at(HALO - 8 + part * which, part)]
        remote(
            there_rows, there_rows, pass_send.at[0], pass_recv.at[which], group
        ).wait_recv()

    def chain(begin, a_ref, b_ref, core, states, edge, steps):
        last = begin
        m = len(begin[0])
        for t in range(steps):
            if t % 4 == 0:
                for n in range(t, min(t + 4, steps)):
                    halo = 24 if n == 0 else 16 if n <= 8 else 8
                    rows = cts.at[n, :, edge - halo : edge + core + halo]

                    @pl.when(n != local_group)
                    def _(n=n, rows=rows):
                        remote(
                            rows, rows, ct_send.at[0], ct_recv.at[n], sibling
                        ).wait_recv()

            last = advance(last, a_ref, b_ref, 64.0 * KAPPA)
            last = plus(last, load_rows(cts.at[t, :, 0 : 8 * m], m))
            store_state(states.at[t + 1], last)
        return last

    @pl.when(jnp.logical_and(core0, stage == 0))
    def _():
        copy_strip(cts.at[local_group], ct_rows.at[:, :], half_first, HALF_ROWS)
        begin = load_rows(half_strip, MH)
        store_state(half_history.at[0], begin)
        last = chain(begin, a_half, b_half, HALF, half_history, EDGE, STAGE)
        store_rows(hop_rows, last)
        for copy in hop:
            copy.start()
        other = (local_group + STAGE // 2) % STAGE
        for n, t in enumerate((local_group + 1, other, other + 1)):
            store_rows(pass_rows.at[n], load_state(half_history.at[t]))
            given[n].start()
        store_rows(half_strip, load_state(half_history.at[local_group]))
        for h in range(2):
            z_in[h, rows_at(half_dst, part)] = half_strip[h, rows_at(half_src, part)]

    @pl.when(jnp.logical_and(core0, stage == 1))
    def _():
        store_rows(cts.at[local_group], load_state(ct))
        for copy in hop_arrivals:
            copy.wait_recv()
        begin = load_rows(z_stage, M)
        store_state(history.at[0], begin)
        chain(begin, a_64, b_64, CORE, history, HALO, STAGE - 1)
        store_rows(pass_rows.at[0], load_state(history.at[local_group + 1]))
        pass_copy.start()
        store_state(z_own, load_state(history.at[local_group]))

    @pl.when(stage == 0)
    def _():
        half_arrived(1 - mine)
        pl.when(c == 1)(lambda: half_arrived(mine))
        store_state(z_own, load_rows(z_in, M))

    @pl.when(jnp.logical_and(c == 1, stage == 1))
    def _():
        pass_copy.wait_recv()
        store_state(z_own, load_rows(z_in, M))

    final = load_state(z_own)
    final = plus(advance(final, a_64, b_64, 64.0 * KAPPA), load_state(ct))
    state = load_state(z_own)
    for index in (3, 0, 1, 2):
        if index < 3:
            state = big_step(state, index)
        store_rows(point_rows.at[index], state if index < 3 else final)

    for d in (2, 1, 3):
        index = around(d)
        copy = pltpu.make_async_remote_copy(
            src_ref=point_rows.at[index, :, core_rows],
            dst_ref=points_full.at[:, own_rows],
            send_sem=point_send.at[d],
            recv_sem=point_recv.at[member],
            device_id=(group, index),
            device_id_type=MESH,
        )
        copy.start()
        pending.append((None, copy))
    for h in range(2):
        points_full[h, own_rows] = point_rows[member, h, core_rows]
    for d in (0, 1, 3, 2):
        q = around(d)
        rows = pl.ds(pl.multiple_of(q * CORE, 8), CORE)
        if d:
            pltpu.make_async_remote_copy(
                src_ref=point_rows.at[0, :, core_rows],
                dst_ref=points_full.at[:, rows],
                send_sem=point_send.at[0],
                recv_sem=point_recv.at[q],
                device_id=(group, q),
                device_id_type=MESH,
            ).wait_recv()
        both = jnp.concatenate([points_full[0, rows], points_full[1, rows]], axis=1)
        points_ref[rows] = permuted(both, perm[...])

    for when, copy in pending:
        if when is None:
            copy.wait_send()
        else:
            pl.when(when)(copy.wait_send)

    for halo, when in widths:
        for of_stage in range(2):

            @pl.when(jnp.logical_and(when, stage == of_stage))
            def _(halo=halo, of_stage=of_stage):
                copies = ct_copies(halo, of_stage)
                for copy in copies[:-1]:
                    copy.wait_send()
                pl.when(c == 1)(copies[-1].wait_send)

    @pl.when(jnp.logical_and(core0, stage == 0))
    def _():
        for copy in hop + given:
            copy.wait_send()

    @pl.when(jnp.logical_and(core0, stage == 1))
    def _():
        pass_copy.wait_send()


def write_out(points, corner, points_out, corner_out, sems):
    copies = (
        pltpu.make_async_copy(points, points_out.at[0], sems.at[0]),
        pltpu.make_async_copy(corner, corner_out.at[0], sems.at[1]),
    )
    for copy in copies:
        copy.start()
    for copy in copies:
        copy.wait()


def local(init_field, reaction, guesses):
    vmem = pl.BlockSpec(memory_space=pltpu.VMEM)
    strip_state = pltpu.VMEM((2, M, 8, LANES), F32)
    full_state = pltpu.VMEM((2, MF, 8, LANES), F32)
    strip_rows = pltpu.VMEM((2, ROWS, LANES), F32)
    ext_rows = pltpu.VMEM((2, N + 2 * HALO, LANES), F32)
    full_rows = pltpu.VMEM((2, N, LANES), F32)
    dma = pltpu.SemaphoreType.DMA

    def many(count, *shape):
        return pltpu.VMEM((count, *shape), F32)

    scratch = [
        *[pltpu.VMEM((N, N), F32)] * 3,
        pltpu.VMEM((N, N), jnp.bfloat16),
        ext_rows,
        ext_rows,
        ext_rows,
        strip_rows,
        full_state,
        full_state,
        *[strip_state] * 6,
        many(4, 2, ROWS, LANES),
        many(4, 2, M, 8, LANES),
        strip_rows,
        full_rows,
        strip_rows,
        strip_rows,
        strip_state,
        many(STAGE, 2, ROWS, LANES),
        many(STAGE + 1, 2, M, 8, LANES),
        many(STAGE + 1, 2, MH, 8, LANES),
        pltpu.VMEM((2, HALF_ROWS, LANES), F32),
        *[pltpu.VMEM((2, MH, 8, LANES), F32)] * 2,
        pltpu.VMEM((2, HALF_ROWS, LANES), F32),
        strip_rows,
        many(3, 2, ROWS, LANES),
        strip_rows,
        strip_state,
        many(4, 2, ROWS, LANES),
        full_rows,
        dma((3,)),
        dma((8,)),
        dma((4, 4)),
        dma((4,)),
        dma((3,)),
        dma((4,)),
        dma((2,)),
        dma((2,)),
        dma((8,)),
        dma((STAGE,)),
        dma((4,)),
        dma((4,)),
        dma((3,)),
        dma((2,)),
        dma((4,)),
        dma((4,)),
    ]
    hbm = pl.BlockSpec(memory_space=pltpu.HBM)
    points, corner = pl.pallas_call(
        kernel,
        out_shape=(
            jax.ShapeDtypeStruct((N, N), F32),
            jax.ShapeDtypeStruct((N, N), F32),
        ),
        in_specs=[hbm] * 3,
        out_specs=(vmem, vmem),
        scratch_shapes=scratch,
        compiler_params=pltpu.CompilerParams(
            collective_id=0, has_side_effects=True, vmem_limit_bytes=213 * 2**18
        ),
    )(init_field, reaction, guesses)
    block = jax.ShapeDtypeStruct((1, N, N), F32)
    return pl.pallas_call(
        write_out,
        out_shape=(block, block),
        in_specs=[vmem] * 2,
        out_specs=(hbm, hbm),
        scratch_shapes=[dma((2,))],
        compiler_params=pltpu.CompilerParams(vmem_limit_bytes=8 * 2**20),
    )(points, corner)


def solution(mesh):
    return jax.shard_map(
        local,
        mesh=mesh,
        in_specs=(P(), P(), P(("tm", "grp"), None, None)),
        out_specs=(P(("tm", "grp"), None, None), P("tm", None, None)),
        check_vma=False,
    )
```
